32 devices in a mesh: grp: 4 (over y, x), row: 8 (over z, core).
Axes of the slice: x: 2, y: 2, z: 4, core: 2. Of those that a mesh axis runs over, the one named last changes fastest.
Arguments:
- coarse_blocks: bfloat16 [2048, 64, 512], P(('grp', 'row'))
- smoother: bfloat16 [2048, 4096], P(('grp', 'row'))
- residual: bfloat16 [2048, 512], P(('grp', 'row')), may hold values from -6 to 6
- dest: int32 [2048, 1], P(('grp', 'row')), may hold values from 0 to 31, as said below
- band_cols: int32 [2048, 8], P(('grp', 'row')), may hold values from 0 to 511, as said below
- band_mask: int32 [2048, 8], P(('grp', 'row')), may hold values from 0 to 1, as said below
Outputs:
- smoothed: float32 [2048, 512], P(('grp', 'row'))
The draws below stay inside these ranges and needn't reach their ends.
Inputs may be any that keep to these rules, and one draw needn't show every extreme that they name: `dest`: at most 2 of the rows of one device have the same owner, and in every draw some owners receive exactly 2 rows from every device. `band_cols`: every entry names the slot index, within the owner's subgroup, of a row whose owner is in the same subgroup: owner's row index * 64 + source device * 2 + its rank among that source's rows to that owner. The first entry names the row itself. `band_mask`: the first entry of every row is 1.
All inputs are finite; a program needn't handle non-finite values.
Results may differ from the reference program's by a relative error of at most 0.0035.
Values may be sent and summed in bfloat16 or wider, within the bound.
No kernel may reach another device: no remote copies, remote signals or barrier semaphores. Data moves between devices by JAX's collectives and lax.ppermute only.
A program may use at most 192 MiB of HBM per device.

```python
import math
import jax
import jax.numpy as jnp
from jax import lax

BS = 64
NB = 8
NRHS = 8
RB_DEV = 64
CAP = 2
SWEEPS = 3
BR = 2048
SLOTS = 64
N_GRP = 4
N_ROW = 8


def routing(key):
    devices = N_GRP * N_ROW
    hot_count = RB_DEV // (2 * CAP)
    ranking = jnp.argsort(jax.random.permutation(jax.random.fold_in(key, 11), devices))
    hot_flag = (ranking < hot_count).astype(jnp.int32)
    tickets = devices * CAP
    ticket_dev = jnp.arange(tickets, dtype=jnp.int32) // CAP
    jitter = jax.random.randint(jax.random.fold_in(key, 12), (devices, tickets), 0, 2 ** 18)
    score = jitter * 1024 + jnp.arange(tickets, dtype=jnp.int32)[None, :] + hot_flag[ticket_dev][None, :] * 2 ** 29
    top_scores, chosen = lax.top_k(score, RB_DEV)
    owners = chosen // CAP
    shuffle = jnp.argsort(jax.random.randint(jax.random.fold_in(key, 13), (devices, RB_DEV), 0, 2 ** 30), axis=1, stable=True)
    owners = jnp.take_along_axis(owners, shuffle, axis=1).astype(jnp.int32)
    onehot = (owners[:, :, None] == jnp.arange(devices, dtype=jnp.int32)[None, None, :]).astype(jnp.int32)
    within = jnp.sum((jnp.cumsum(onehot, axis=1) - 1) * onehot, axis=2).reshape(-1)
    target = owners.reshape(-1)
    source = jnp.arange(BR, dtype=jnp.int32) // RB_DEV
    local_slot = target % N_ROW * SLOTS + source * CAP + within
    subgroup = target // N_ROW
    sorted_rows = jnp.argsort(subgroup, stable=True)
    counts = jnp.sum((subgroup[:, None] == jnp.arange(N_GRP, dtype=jnp.int32)[None, :]).astype(jnp.int32), axis=0)
    starts = jnp.cumsum(counts) - counts
    chosen_pos = jax.random.randint(jax.random.fold_in(key, 14), (BR, NB - 1), 0, 2 ** 20) % counts[subgroup][:, None] + starts[subgroup][:, None]
    partner = sorted_rows[chosen_pos]
    columns = jnp.concatenate([local_slot[:, None], local_slot[partner]], axis=1).astype(jnp.int32)
    coin_bits = jax.random.randint(jax.random.fold_in(key, 15), (BR, NB - 1), 0, 2)
    hot_row = hot_flag[target][:, None]
    live_mask = jnp.concatenate([jnp.ones((BR, 1), jnp.int32), jnp.maximum(coin_bits, hot_row)], axis=1).astype(jnp.int32)
    return (target[:, None].astype(jnp.int32), columns, live_mask)


def draw_dest(key, part):
    return routing(key)[0]


def draw_band_cols(key, part):
    return routing(key)[1]


def draw_band_mask(key, part):
    return routing(key)[2]


def draw_coarse_blocks(key, part):
    key = jax.random.fold_in(key, 21)
    shape = (BR, BS, NB * BS)
    jitter = jax.random.normal(key, shape, jnp.float32)
    column = lax.broadcasted_iota(jnp.int32, shape, 2)
    inner = lax.broadcasted_iota(jnp.int32, shape, 1)
    diagonal = (column == inner).astype(jnp.float32)
    first = (column < BS).astype(jnp.float32)
    spread = (first * 0.3 + (1.0 - first) * 0.35) / math.sqrt(BS)
    return (2.0 * diagonal + spread * jitter).astype(jnp.bfloat16)


def draw_smoother(key, part):
    key = jax.random.fold_in(key, 22)
    shape = (BR, BS * BS)
    jitter = jax.random.normal(key, shape, jnp.float32)
    flat = lax.broadcasted_iota(jnp.int32, shape, 1)
    diagonal = (flat // BS == flat % BS).astype(jnp.float32)
    return (0.5 * diagonal + 0.08 / math.sqrt(BS) * jitter).astype(jnp.bfloat16)


def steps_of(stream_key, shape, split, least, largest):
    gain, own = 1.0, jax.random.fold_in(stream_key, 6)
    for dim, blocks in split:
        draws = jnp.exp(jax.random.uniform(jax.random.fold_in(own, dim), (blocks,), jnp.float32, least / len(split), largest / len(split)))
        gain = gain * jnp.repeat(draws, shape[dim] // blocks).reshape([-1 if axis == dim else 1 for axis in range(len(shape))])
    return gain


def gaussian(rng, shape, scale, most, cuts=(), kind=jnp.bfloat16):
    values = scale * jax.random.normal(rng, shape, jnp.float32)
    if cuts:
        values = values * steps_of(rng, shape, cuts, -0.22, 0.18)
    return jnp.clip(values, -most, most).astype(kind)


def setup_inputs(seed: int = 0) -> dict:
    seeds = jax.random.split(jax.random.key(seed), 7)
    coarse_blocks = draw_coarse_blocks(jax.random.fold_in(seeds[6], 71), 0)
    smoother = draw_smoother(jax.random.fold_in(seeds[6], 71), 0)
    residual = gaussian(seeds[2], (BR, NRHS * BS), 1.0, 6.0, ((0, 32),))
    dest = draw_dest(jax.random.fold_in(seeds[6], 71), 0)
    band_cols = draw_band_cols(jax.random.fold_in(seeds[6], 71), 0)
    band_mask = draw_band_mask(jax.random.fold_in(seeds[6], 71), 0)
    return {"coarse_blocks": coarse_blocks, "smoother": smoother, "residual": residual, "dest": dest, "band_cols": band_cols, "band_mask": band_mask}


def reference(coarse_blocks, smoother, residual, dest, band_cols, band_mask):
    devices = N_GRP * N_ROW
    target = dest[:, 0]
    grouped = target.reshape(devices, RB_DEV)
    onehot = (grouped[:, :, None] == jnp.arange(devices, dtype=jnp.int32)[None, None, :]).astype(jnp.int32)
    within = jnp.sum((jnp.cumsum(onehot, axis=1) - 1) * onehot, axis=2).reshape(-1).astype(jnp.int32)
    source = (jnp.arange(BR, dtype=jnp.int32) // RB_DEV).astype(jnp.int32)
    placed = (target * SLOTS + source * CAP + within).astype(jnp.int32)
    lookup = jnp.zeros((devices * SLOTS,), jnp.int32).at[placed].set(jnp.arange(BR, dtype=jnp.int32))
    group_base = ((target // N_ROW) * (N_ROW * SLOTS)).astype(jnp.int32)
    neighbour = lookup[group_base[:, None] + band_cols]
    keep_mask = band_mask.astype(jnp.bfloat16)
    blocks = coarse_blocks.reshape(BR, BS, NB, BS) * keep_mask[:, None, :, None]
    block_groups = blocks.reshape(devices, RB_DEV, BS, NB, BS)
    index_groups = neighbour.reshape(devices, RB_DEV, NB)
    smooth = smoother.reshape(BR, BS, BS).astype(jnp.float32)
    right_side = residual.reshape(BR, NRHS, BS).astype(jnp.float32)
    solution = jnp.zeros((BR, NRHS, BS), jnp.float32)
    for sweep_index in range(SWEEPS):
        rounded = lax.optimization_barrier(solution.astype(jnp.bfloat16)).astype(jnp.float32)

        def apply_band(pieces):
            block_part, index_part = pieces
            values = rounded[index_part]
            return jnp.einsum('sibk,sbrk->sri', block_part.astype(jnp.float32), values)

        applied = lax.map(apply_band, (block_groups, index_groups)).reshape(BR, NRHS, BS)
        defect = lax.optimization_barrier((right_side - applied).astype(jnp.bfloat16)).astype(jnp.float32)
        solution = solution + jnp.einsum('sik,srk->sri', smooth, defect)
    output = jnp.zeros((devices * SLOTS, NRHS * BS), jnp.float32)
    return output.at[placed].set(solution.reshape(BR, NRHS * BS))
```

```python
import functools

import jax
import jax.numpy as jnp
from jax import lax
from jax.experimental import pallas as pl
from jax.experimental.pallas import tpu as pltpu
from jax.sharding import PartitionSpec as P

NRHS = 8
CAP = 2
LANES = 128
CHUNKS = 4
VMEM_LIMIT = 48 * 1024 * 1024

TRANSPOSED = (((1,), (1,)), ((), ()))


def first_sweep(full, dest_ref, smooth_ref, right_ref, perm_ref, starts_ref, x_ref, xb_ref, rp_ref, sbd_ref, count):
    rows = dest_ref.shape[0]
    owners = starts_ref.shape[0]
    pairs = x_ref.shape[0]
    block = smooth_ref.shape[1]

    def clear(owner, carry):
        count[owner] = 0
        return carry

    lax.fori_loop(0, owners, clear, 0)
    if full:

        def start(owner, carry):
            starts_ref[owner] = owner * CAP
            return carry

        lax.fori_loop(0, owners, start, 0)
    else:

        def tally(row, carry):
            count[dest_ref[row]] = count[dest_ref[row]] + 1
            return carry

        lax.fori_loop(0, rows, tally, 0)

        def start(owner, total):
            starts_ref[owner] = total
            following = total + count[owner]
            count[owner] = 0
            return following

        lax.fori_loop(0, owners, start, jnp.int32(0))

    def place(row, carry):
        owner = dest_ref[row]
        rank = count[owner]
        count[owner] = rank + 1
        perm_ref[starts_ref[owner] + rank] = row
        return carry

    lax.fori_loop(0, rows, place, 0)

    zero = jnp.zeros((block, block), jnp.bfloat16)
    for pair in range(pairs):
        low, high = perm_ref[2 * pair], perm_ref[2 * pair + 1]
        both = jnp.concatenate(
            [
                jnp.concatenate([smooth_ref[low], zero], axis=1),
                jnp.concatenate([zero, smooth_ref[high]], axis=1),
            ],
            axis=0,
        )
        right = jnp.concatenate([right_ref[low], right_ref[high]], axis=1)
        x = lax.dot_general(right, both, TRANSPOSED, preferred_element_type=jnp.float32)
        sbd_ref[pair] = both
        rp_ref[pair] = right
        x_ref[pair] = x
        xb_ref[pair] = x.astype(jnp.bfloat16)


def later_sweep(piece_count, with_rounded, *refs):
    perm_ref, index_ref = refs[:2]
    pieces = refs[2 : 2 + piece_count]
    blocks_hbm, sbd_ref, rp_ref, x_ref = refs[2 + piece_count : 6 + piece_count]
    refs = refs[6 + piece_count :]
    out_ref = refs[0]
    rounded_ref = refs[1] if with_rounded else None
    tiles, blocks, tile_sem, block_sem = refs[2 if with_rounded else 1 :]
    pairs = x_ref.shape[0]
    rows, block, width = blocks.shape
    bands = width // block
    piece_tiles = pieces[0].shape[0]
    part = rows // CHUNKS

    tile_copies = [
        pltpu.make_async_copy(piece, tiles.at[pl.ds(number * piece_tiles, piece_tiles)], tile_sem.at[number])
        for number, piece in enumerate(pieces)
    ]
    block_copies = [
        pltpu.make_async_copy(
            blocks_hbm.at[pl.ds(number * part, part)], blocks.at[pl.ds(number * part, part)], block_sem.at[number]
        )
        for number in range(CHUNKS)
    ]
    for copy in tile_copies + block_copies:
        copy.start()
    tiles[piece_count * piece_tiles] = jnp.zeros((NRHS, LANES), jnp.bfloat16)
    for copy in tile_copies + block_copies:
        copy.wait()

    lower = lax.broadcasted_iota(jnp.int32, (NRHS, LANES), 1) < block

    def fetch(row, band):
        entry = index_ref[row * bands + band]
        tile = tiles[lax.shift_right_logical(entry, 1)].astype(jnp.float32)
        return pltpu.roll(tile, (entry & 1) * block, 1)

    def values(row):
        return [
            jnp.where(lower, fetch(row, 2 * half), fetch(row, 2 * half + 1)) for half in range(bands // 2)
        ]

    for pair in range(pairs):
        low, high = perm_ref[2 * pair], perm_ref[2 * pair + 1]
        gathered = jnp.concatenate(
            [
                jnp.concatenate(values(low), axis=1),
                jnp.concatenate(values(high), axis=1),
            ],
            axis=0,
        ).astype(jnp.bfloat16)
        weights = jnp.concatenate([blocks[low], blocks[high]], axis=0)
        applied = lax.dot_general(gathered, weights, TRANSPOSED, preferred_element_type=jnp.float32)
        image = jnp.where(lower, applied[:NRHS], applied[NRHS:])
        defect = (rp_ref[pair].astype(jnp.float32) - image).astype(jnp.bfloat16)
        x = x_ref[pair] + lax.dot_general(
            defect, sbd_ref[pair], TRANSPOSED, preferred_element_type=jnp.float32
        )
        out_ref[pair] = x
        if with_rounded:
            rounded_ref[pair] = x.astype(jnp.bfloat16)


def local(coarse_blocks, smoother, residual, dest, band_cols, band_mask):
    groups = lax.axis_size("grp")
    members = lax.axis_size("row")
    devices = groups * members
    rows, block, width = coarse_blocks.shape
    bands = band_cols.shape[1]
    pairs = rows // 2
    full = rows == devices * CAP
    smem = pl.BlockSpec(memory_space=pltpu.SMEM)
    vmem = pl.BlockSpec(memory_space=pltpu.VMEM)
    anywhere = pl.BlockSpec(memory_space=pl.ANY)
    tile_shape = (pairs, NRHS, LANES)
    params = pltpu.CompilerParams(vmem_limit_bytes=VMEM_LIMIT)

    perm, starts, x, rounded, right, smooth = pl.pallas_call(
        functools.partial(first_sweep, full),
        out_shape=(
            jax.ShapeDtypeStruct((rows,), jnp.int32),
            jax.ShapeDtypeStruct((devices,), jnp.int32),
            jax.ShapeDtypeStruct(tile_shape, jnp.float32),
            jax.ShapeDtypeStruct(tile_shape, jnp.bfloat16),
            jax.ShapeDtypeStruct(tile_shape, jnp.bfloat16),
            jax.ShapeDtypeStruct((pairs, 2 * block, 2 * block), jnp.bfloat16),
        ),
        in_specs=[smem, vmem, vmem],
        out_specs=(smem, smem, vmem, vmem, vmem, vmem),
        scratch_shapes=[pltpu.SMEM((devices,), jnp.int32)],
        compiler_params=params,
        name="first_sweep",
    )(dest.reshape(rows), smoother.reshape(rows, block, block), residual.reshape(rows, NRHS, block))

    row_bits = [1 << bit for bit in range(members.bit_length() - 2, 0, -1)]
    slots = devices * CAP
    member = band_cols // slots
    source = (band_cols % slots) // CAP
    rank = band_cols % CAP
    owner = (dest // members) * members + member
    if full:
        position = owner * CAP + rank
    else:
        table = lax.all_gather(starts, ("grp", "row"), axis=0, tiled=True)
        position = jnp.take(table, source * devices + owner, mode="clip") + rank
    relative_row = (source % members) ^ lax.axis_index("row")
    relative_group = (source // members) ^ lax.axis_index("grp")
    piece = (relative_row & 1) * groups + relative_group
    within = jnp.zeros_like(piece)
    for order, bit in enumerate(row_bits):
        within = within + ((relative_row // bit) & 1) * (1 << order)
    tile = (piece * (members // 2) + within) * pairs + position // 2
    swap = (position ^ jnp.arange(bands, dtype=jnp.int32)[None, :]) & 1
    dead = devices * pairs
    index = jnp.where(band_mask != 0, tile * 2 + swap, dead * 2).reshape(rows * bands)

    def exchange(value, axis, size, distance):
        return lax.ppermute(value, axis, [(place, place ^ distance) for place in range(size)])

    def everywhere(value):
        for bit in row_bits:
            value = jnp.concatenate([value, exchange(value, "row", members, bit)], axis=0)
        near = [value] + [exchange(value, "grp", groups, distance) for distance in range(1, groups)]
        return near + [exchange(part, "row", members, 1) for part in near]

    def sweep(x, rounded, last):
        pieces = everywhere(rounded)
        outs = [jax.ShapeDtypeStruct(tile_shape, jnp.float32)]
        if not last:
            outs.append(jax.ShapeDtypeStruct(tile_shape, jnp.bfloat16))
        return pl.pallas_call(
            functools.partial(later_sweep, len(pieces), not last),
            out_shape=tuple(outs),
            in_specs=[smem, smem] + [anywhere] * (len(pieces) + 1) + [vmem] * 3,
            out_specs=tuple([vmem] * len(outs)),
            scratch_shapes=[
                pltpu.VMEM((devices * pairs + 1, NRHS, LANES), jnp.bfloat16),
                pltpu.VMEM((rows, block, width), jnp.bfloat16),
                pltpu.SemaphoreType.DMA((len(pieces),)),
                pltpu.SemaphoreType.DMA((CHUNKS,)),
            ],
            compiler_params=params,
            name="later_sweep",
        )(perm, index, *pieces, coarse_blocks, smooth, right, x)

    x, rounded = sweep(x, rounded, False)
    (x,) = sweep(x, rounded, True)

    if not full:
        flat = x.reshape(pairs, NRHS, 2, block).transpose(0, 2, 1, 3).reshape(rows, NRHS * block)
        following = jnp.concatenate([starts[1:], jnp.full((1,), rows, jnp.int32)])
        wanted = starts[:, None] + jnp.arange(CAP, dtype=jnp.int32)[None, :]
        live = wanted < following[:, None]
        flat = jnp.where(
            live.reshape(slots, 1), jnp.take(flat, wanted.reshape(slots), axis=0, mode="clip"), 0.0
        )
        x = flat.reshape(devices, CAP, NRHS, block).transpose(0, 2, 1, 3).reshape(devices, NRHS, CAP * block)
    got = lax.all_to_all(x, ("grp", "row"), split_axis=0, concat_axis=0, tiled=True)
    got = got.reshape(devices, NRHS, CAP, block).transpose(0, 2, 1, 3)
    return got.reshape(slots, NRHS * block)


def solution(mesh):
    in_specs = (
        P(("grp", "row"), None, None),
        P(("grp", "row"), None),
        P(("grp", "row"), None),
        P(("grp", "row"), None),
        P(("grp", "row"), None),
        P(("grp", "row"), None),
    )
    out_specs = P(("grp", "row"), None)
    return jax.shard_map(local, mesh=mesh, in_specs=in_specs, out_specs=out_specs, check_vma=False)
```

```python
import functools

import jax
import jax.numpy as jnp
from jax import lax
from jax.experimental import pallas as pl
from jax.experimental.pallas import tpu as pltpu
from jax.sharding import PartitionSpec as P

NRHS = 8
CAP = 2
LANES = 128
VMEM_LIMIT = 32 * 1024 * 1024

TRANSPOSED = (((1,), (1,)), ((), ()))
PLAIN = (((1,), (0,)), ((), ()))
SUB = 8


def spread_rows(source_ref, spread_ref, copies):
    rows, width = source_ref.shape
    tiles = width // LANES
    for top in range(rows // SUB):
        values = source_ref[top * SUB : (top + 1) * SUB, :].astype(jnp.float32)
        for place, (tile, turned) in enumerate(copies):
            piece = values[:, tile * LANES : (tile + 1) * LANES]
            if turned:
                piece = pltpu.roll(piece, LANES // 2, 1)
            spread_ref[pl.ds((top * len(copies) + place) * SUB, SUB), :] = piece


def spread_row(spread_ref, row, tiles, first, count):
    start = (row // SUB) * (tiles * SUB) + first * SUB + row % SUB
    return spread_ref[pl.ds(start, count, stride=SUB), :]


def smooth_copies(width):
    return [(tile, False) for tile in range(width // LANES)]


def right_copies(width):
    plain = [(tile, False) for tile in range(width // LANES)]
    turned = [(tile, True) for tile in range(width // LANES)]
    return plain + turned + plain


def sort_rows(full, dest_ref, perm_ref, starts_ref, count):
    rows = dest_ref.shape[0]
    owners = starts_ref.shape[0]
    if full:
        for owner in range(owners):
            count[owner] = owner * CAP
            starts_ref[owner] = owner * CAP
    else:

        def clear(owner, carry):
            count[owner] = 0
            return carry

        lax.fori_loop(0, owners, clear, 0)

        def tally(row, carry):
            count[dest_ref[row]] = count[dest_ref[row]] + 1
            return carry

        lax.fori_loop(0, rows, tally, 0)

        def start(owner, total):
            following = total + count[owner]
            starts_ref[owner] = total
            count[owner] = total
            return following

        lax.fori_loop(0, owners, start, jnp.int32(0))
    for row in range(rows):
        owner = dest_ref[row]
        position = count[owner]
        count[owner] = position + 1
        perm_ref[position] = row


def first_sweep(
    full, dest_hbm, smooth_hbm, right_hbm, perm_ref, starts_ref, xb_ref,
    dest_ref, count, smooth_ref, right_ref, smooth_spread, right_spread, collected, sems,
):
    copies = [
        pltpu.make_async_copy(dest_hbm, dest_ref, sems.at[0]),
        pltpu.make_async_copy(right_hbm, right_ref, sems.at[1]),
        pltpu.make_async_copy(smooth_hbm, smooth_ref, sems.at[2]),
    ]
    for copy in copies:
        copy.start()
    rows, smooth_width = smooth_ref.shape
    block = LANES // 2
    half = smooth_width // LANES
    quad = LANES // half
    lanes = lax.broadcasted_iota(jnp.int32, (2 * SUB, LANES), 1)
    lower = lanes[:SUB] < block
    width = quad * block
    held = lax.broadcasted_iota(jnp.int32, (width, width), 0)
    wanted = lax.broadcasted_iota(jnp.int32, (width, width), 1)
    placed = ((held % LANES) // half) * block + 2 * (held % half) + held // LANES
    order = jnp.where(placed == wanted, 1.0, 0.0).astype(jnp.bfloat16)

    copies[0].wait()
    sort_rows(full, dest_ref, perm_ref, starts_ref, count)
    copies[1].wait()
    copied = right_copies(right_ref.shape[1])
    spread_rows(right_ref, right_spread, copied)
    copies[2].wait()
    spread_rows(smooth_ref, smooth_spread, smooth_copies(smooth_width))

    for group in range(rows // quad):
        weights, values = [], []
        for member in range(quad):
            row = perm_ref[quad * group + member]
            weights.append(spread_row(smooth_spread, row, half, 0, half))
            straight = spread_row(right_spread, row, len(copied), 0, SUB)
            crossed = spread_row(right_spread, row, len(copied), SUB // 2, SUB)
            values += [jnp.where(lower, straight, 0.0), jnp.where(lower, 0.0, crossed)]
        products = lax.dot_general(
            jnp.concatenate(values, axis=0).astype(jnp.bfloat16),
            jnp.concatenate(weights, axis=0).astype(jnp.bfloat16),
            TRANSPOSED,
            preferred_element_type=jnp.float32,
        )
        own = products[: 2 * SUB]
        for member in range(1, quad):
            own = jnp.where(
                lanes // half == member, products[2 * SUB * member : 2 * SUB * (member + 1)], own
            )
        collected[pl.ds(group * SUB, SUB), :LANES] = own[:SUB]
        collected[pl.ds(group * SUB, SUB), LANES:] = own[SUB:]
    ordered = lax.dot_general(
        collected[...].astype(jnp.bfloat16), order, PLAIN, preferred_element_type=jnp.float32
    ).astype(jnp.bfloat16)
    for group in range(rows // quad):
        for pair in range(quad // 2):
            xb_ref[group * (quad // 2) + pair] = ordered[
                group * SUB : (group + 1) * SUB, pair * LANES : (pair + 1) * LANES
            ]


def prepare(
    perm_ref, smooth_hbm, right_hbm, blocks_hbm, x_ref, rp_ref, sbd_ref, blocks_ref,
    smooth_ref, right_ref, smooth_spread, right_spread, widened, sems,
):
    copies = [
        pltpu.make_async_copy(right_hbm, right_ref, sems.at[0]),
        pltpu.make_async_copy(smooth_hbm, smooth_ref, sems.at[1]),
        pltpu.make_async_copy(blocks_hbm, blocks_ref, sems.at[2]),
    ]
    for copy in copies:
        copy.start()
    rows, smooth_width = smooth_ref.shape
    block = LANES // 2
    half = smooth_width // LANES
    pairs = rows // 2
    lower = lax.broadcasted_iota(jnp.int32, (SUB, LANES), 1) < block
    low_half = lax.broadcasted_iota(jnp.int32, (half, LANES), 1) < block
    copies[0].wait()
    copied = right_copies(right_ref.shape[1])
    spread_rows(right_ref, right_spread, copied)
    copies[1].wait()
    spread_rows(smooth_ref, smooth_spread, smooth_copies(smooth_width))
    for pair in range(pairs):
        low, high = perm_ref[2 * pair], perm_ref[2 * pair + 1]
        rp_ref[pair] = jnp.where(
            lower,
            spread_row(right_spread, low, len(copied), 0, SUB),
            spread_row(right_spread, high, len(copied), SUB // 2, SUB),
        ).astype(jnp.bfloat16)
        base = pair * LANES
        for number, row in enumerate((low, high)):
            straight = spread_row(smooth_spread, row, half, 0, half)
            turned = pltpu.roll(straight, block, 1)
            first, second = (straight, turned) if number == 0 else (turned, straight)
            keep = low_half if number == 0 else jnp.logical_not(low_half)
            widened[pl.ds(base + number * block, half, stride=2), :] = jnp.where(keep, first, 0.0)
            widened[pl.ds(base + number * block + 1, half, stride=2), :] = jnp.where(keep, second, 0.0)
    for pair in range(pairs):
        sbd_ref[pair] = widened[pl.ds(pair * LANES, LANES), :].astype(jnp.bfloat16)
    for pair in range(pairs):
        x_ref[pair] = lax.dot_general(
            rp_ref[pair], sbd_ref[pair], TRANSPOSED, preferred_element_type=jnp.float32
        )
    copies[2].wait()


def later_sweep(piece_count, with_rounded, *refs):
    perm_ref, index_ref = refs[:2]
    pieces = refs[2 : 2 + piece_count]
    blocks, sbd_ref, rp_ref, x_ref = refs[2 + piece_count : 6 + piece_count]
    refs = refs[6 + piece_count :]
    out_ref = refs[0]
    rounded_ref = refs[1] if with_rounded else None
    tiles, defects, tile_sem = refs[2 if with_rounded else 1 :]
    pairs = x_ref.shape[0]
    _, block, width = blocks.shape
    bands = width // block
    piece_tiles = pieces[0].shape[0]

    tile_copies = [
        pltpu.make_async_copy(piece, tiles.at[pl.ds(number * piece_tiles, piece_tiles)], tile_sem.at[number])
        for number, piece in enumerate(pieces)
    ]
    for copy in tile_copies:
        copy.start()
    tiles[piece_count * piece_tiles] = jnp.zeros((NRHS, LANES), jnp.bfloat16)
    for copy in tile_copies:
        copy.wait()

    lower = lax.broadcasted_iota(jnp.int32, (NRHS, LANES), 1) < block

    def fetch(row, band):
        entry = index_ref[row * bands + band]
        tile = tiles[lax.shift_right_logical(entry, 1)].astype(jnp.float32)
        return pltpu.roll(tile, (entry & 1) * block, 1)

    def values(row):
        return [
            jnp.where(lower, fetch(row, 2 * half), fetch(row, 2 * half + 1)) for half in range(bands // 2)
        ]

    for pair in range(pairs):
        low, high = perm_ref[2 * pair], perm_ref[2 * pair + 1]
        gathered = jnp.concatenate(
            [
                jnp.concatenate(values(low), axis=1),
                jnp.concatenate(values(high), axis=1),
            ],
            axis=0,
        ).astype(jnp.bfloat16)
        weights = jnp.concatenate([blocks[low], blocks[high]], axis=0)
        applied = lax.dot_general(gathered, weights, TRANSPOSED, preferred_element_type=jnp.float32)
        image = jnp.where(lower, applied[:NRHS], applied[NRHS:])
        defects[pair] = (rp_ref[pair].astype(jnp.float32) - image).astype(jnp.bfloat16)

    for pair in range(pairs):
        x = x_ref[pair] + lax.dot_general(
            defects[pair], sbd_ref[pair], TRANSPOSED, preferred_element_type=jnp.float32
        )
        out_ref[pair] = x
        if with_rounded:
            rounded_ref[pair] = x.astype(jnp.bfloat16)


def local(coarse_blocks, smoother, residual, dest, band_cols, band_mask):
    groups = lax.axis_size("grp")
    members = lax.axis_size("row")
    devices = groups * members
    rows, block, width = coarse_blocks.shape
    bands = band_cols.shape[1]
    pairs = rows // 2
    full = rows == devices * CAP
    smem = pl.BlockSpec(memory_space=pltpu.SMEM)
    vmem = pl.BlockSpec(memory_space=pltpu.VMEM)
    anywhere = pl.BlockSpec(memory_space=pl.ANY)
    tile_shape = (pairs, NRHS, LANES)
    params = pltpu.CompilerParams(vmem_limit_bytes=VMEM_LIMIT)

    smooth_width, right_width = smoother.shape[1], residual.shape[1]
    smooth_rows = rows * len(smooth_copies(smooth_width))
    right_rows = rows * len(right_copies(right_width))
    perm, starts, rounded = pl.pallas_call(
        functools.partial(first_sweep, full),
        out_shape=(
            jax.ShapeDtypeStruct((rows,), jnp.int32),
            jax.ShapeDtypeStruct((devices,), jnp.int32),
            jax.ShapeDtypeStruct(tile_shape, jnp.bfloat16),
        ),
        in_specs=[anywhere] * 3,
        out_specs=(smem, smem, vmem),
        scratch_shapes=[
            pltpu.SMEM((rows,), jnp.int32),
            pltpu.SMEM((devices,), jnp.int32),
            pltpu.VMEM(smoother.shape, jnp.bfloat16),
            pltpu.VMEM(residual.shape, jnp.bfloat16),
            pltpu.VMEM((smooth_rows, LANES), jnp.float32),
            pltpu.VMEM((right_rows, LANES), jnp.float32),
            pltpu.VMEM((pairs * SUB // 2, 2 * LANES), jnp.float32),
            pltpu.SemaphoreType.DMA((3,)),
        ],
        compiler_params=params,
        name="first_sweep",
    )(dest.reshape(rows), smoother, residual)
    x, right, smooth, blocks = pl.pallas_call(
        prepare,
        out_shape=(
            jax.ShapeDtypeStruct(tile_shape, jnp.float32),
            jax.ShapeDtypeStruct(tile_shape, jnp.bfloat16),
            jax.ShapeDtypeStruct((pairs, 2 * block, 2 * block), jnp.bfloat16),
            jax.ShapeDtypeStruct(coarse_blocks.shape, jnp.bfloat16),
        ),
        in_specs=[smem] + [anywhere] * 3,
        out_specs=(vmem,) * 4,
        scratch_shapes=[
            pltpu.VMEM(smoother.shape, jnp.bfloat16),
            pltpu.VMEM(residual.shape, jnp.bfloat16),
            pltpu.VMEM((smooth_rows, LANES), jnp.float32),
            pltpu.VMEM((right_rows, LANES), jnp.float32),
            pltpu.VMEM((pairs * LANES, LANES), jnp.float32),
            pltpu.SemaphoreType.DMA((3,)),
        ],
        compiler_params=params,
        name="prepare",
    )(perm, smoother, residual, coarse_blocks)

    row_bits = [1 << bit for bit in range(members.bit_length() - 2, 0, -1)]
    slots = devices * CAP
    member = band_cols // slots
    source = (band_cols % slots) // CAP
    rank = band_cols % CAP
    owner = (dest // members) * members + member
    if full:
        position = owner * CAP + rank
    else:
        table = lax.all_gather(starts, ("grp", "row"), axis=0, tiled=True)
        position = jnp.take(table, source * devices + owner, mode="clip") + rank
    relative_row = (source % members) ^ lax.axis_index("row")
    relative_group = (source // members) ^ lax.axis_index("grp")
    piece = (relative_row & 1) * groups + relative_group
    within = jnp.zeros_like(piece)
    for order, bit in enumerate(row_bits):
        within = within + ((relative_row // bit) & 1) * (1 << order)
    tile = (piece * (members // 2) + within) * pairs + position // 2
    swap = (position ^ jnp.arange(bands, dtype=jnp.int32)[None, :]) & 1
    dead = devices * pairs
    index = jnp.where(band_mask != 0, tile * 2 + swap, dead * 2).reshape(rows * bands)

    def exchange(value, axis, size, distance):
        return lax.ppermute(value, axis, [(place, place ^ distance) for place in range(size)])

    def everywhere(value):
        for bit in row_bits:
            value = jnp.concatenate([value, exchange(value, "row", members, bit)], axis=0)
        near = [value] + [exchange(value, "grp", groups, distance) for distance in range(1, groups)]
        return near + [exchange(part, "row", members, 1) for part in near]

    def sweep(x, rounded, last):
        pieces = everywhere(rounded)
        outs = [jax.ShapeDtypeStruct(tile_shape, jnp.float32)]
        if not last:
            outs.append(jax.ShapeDtypeStruct(tile_shape, jnp.bfloat16))
        return pl.pallas_call(
            functools.partial(later_sweep, len(pieces), not last),
            out_shape=tuple(outs),
            in_specs=[smem, smem] + [anywhere] * len(pieces) + [vmem] * 4,
            out_specs=tuple([vmem] * len(outs)),
            scratch_shapes=[
                pltpu.VMEM((devices * pairs + 1, NRHS, LANES), jnp.bfloat16),
                pltpu.VMEM(tile_shape, jnp.bfloat16),
                pltpu.SemaphoreType.DMA((len(pieces),)),
            ],
            compiler_params=params,
            name="later_sweep",
        )(perm, index, *pieces, blocks, smooth, right, x)

    x, rounded = sweep(x, rounded, False)
    (x,) = sweep(x, rounded, True)

    if not full:
        flat = x.reshape(pairs, 2, NRHS // 2, 2, block).transpose(0, 3, 2, 1, 4).reshape(rows, NRHS * block)
        following = jnp.concatenate([starts[1:], jnp.full((1,), rows, jnp.int32)])
        wanted = starts[:, None] + jnp.arange(CAP, dtype=jnp.int32)[None, :]
        live = wanted < following[:, None]
        flat = jnp.where(
            live.reshape(slots, 1), jnp.take(flat, wanted.reshape(slots), axis=0, mode="clip"), 0.0
        )
        x = flat.reshape(devices, CAP, NRHS // 2, 2, block).transpose(0, 3, 2, 1, 4)
        x = x.reshape(devices, NRHS, CAP * block)
    got = lax.all_to_all(x, ("grp", "row"), split_axis=0, concat_axis=0, tiled=True)
    got = got.reshape(devices, 2, NRHS // 2, CAP, block).transpose(0, 3, 2, 1, 4)
    return got.reshape(slots, NRHS * block)


def solution(mesh):
    in_specs = (
        P(("grp", "row"), None, None),
        P(("grp", "row"), None),
        P(("grp", "row"), None),
        P(("grp", "row"), None),
        P(("grp", "row"), None),
        P(("grp", "row"), None),
    )
    out_specs = P(("grp", "row"), None)
    return jax.shard_map(local, mesh=mesh, in_specs=in_specs, out_specs=out_specs, check_vma=False)
```

```python
import functools

import jax
import jax.numpy as jnp
from jax import lax
from jax.experimental import pallas as pl
from jax.experimental.pallas import tpu as pltpu
from jax.sharding import PartitionSpec as P

NRHS = 8
CAP = 2
LANES = 128
VMEM_LIMIT = 32 * 1024 * 1024

TRANSPOSED = (((1,), (1,)), ((), ()))
PLAIN = (((1,), (0,)), ((), ()))
SUB = 8


def spread_rows(source_ref, spread_ref, copies):
    rows, width = source_ref.shape
    tiles = width // LANES
    for top in range(rows // SUB):
        values = source_ref[top * SUB : (top + 1) * SUB, :].astype(jnp.float32)
        for place, (tile, turned) in enumerate(copies):
            piece = values[:, tile * LANES : (tile + 1) * LANES]
            if turned:
                piece = pltpu.roll(piece, LANES // 2, 1)
            spread_ref[pl.ds((top * len(copies) + place) * SUB, SUB), :] = piece


def spread_row(spread_ref, row, tiles, first, count):
    start = (row // SUB) * (tiles * SUB) + first * SUB + row % SUB
    return spread_ref[pl.ds(start, count, stride=SUB), :]


def smooth_copies(width):
    return [(tile, False) for tile in range(width // LANES)]


def right_copies(width):
    plain = [(tile, False) for tile in range(width // LANES)]
    turned = [(tile, True) for tile in range(width // LANES)]
    return plain + turned + plain


def sort_rows(full, dest_ref, perm_ref, starts_ref, count):
    rows = dest_ref.shape[0]
    owners = starts_ref.shape[0]
    if full:
        for owner in range(owners):
            count[owner] = owner * CAP
            starts_ref[owner] = owner * CAP
    else:

        def clear(owner, carry):
            count[owner] = 0
            return carry

        lax.fori_loop(0, owners, clear, 0)

        def tally(row, carry):
            count[dest_ref[row]] = count[dest_ref[row]] + 1
            return carry

        lax.fori_loop(0, rows, tally, 0)

        def start(owner, total):
            following = total + count[owner]
            starts_ref[owner] = total
            count[owner] = total
            return following

        lax.fori_loop(0, owners, start, jnp.int32(0))
    for row in range(rows):
        owner = dest_ref[row]
        position = count[owner]
        count[owner] = position + 1
        perm_ref[position] = row


def first_sweep(
    full, dest_hbm, smooth_hbm, right_hbm, perm_ref, starts_ref, xb_ref,
    dest_ref, count, smooth_ref, right_ref, smooth_spread, right_spread, collected, sems,
):
    copies = [
        pltpu.make_async_copy(dest_hbm, dest_ref, sems.at[0]),
        pltpu.make_async_copy(right_hbm, right_ref, sems.at[1]),
        pltpu.make_async_copy(smooth_hbm, smooth_ref, sems.at[2]),
    ]
    for copy in copies:
        copy.start()
    rows, smooth_width = smooth_ref.shape
    block = LANES // 2
    half = smooth_width // LANES
    quad = LANES // half
    lanes = lax.broadcasted_iota(jnp.int32, (2 * SUB, LANES), 1)
    lower = lanes[:SUB] < block
    width = quad * block
    held = lax.broadcasted_iota(jnp.int32, (width, width), 0)
    wanted = lax.broadcasted_iota(jnp.int32, (width, width), 1)
    placed = ((held % LANES) // half) * block + 2 * (held % half) + held // LANES
    order = jnp.where(placed == wanted, 1.0, 0.0).astype(jnp.bfloat16)

    copies[0].wait()
    sort_rows(full, dest_ref, perm_ref, starts_ref, count)
    copies[1].wait()
    copied = right_copies(right_ref.shape[1])
    spread_rows(right_ref, right_spread, copied)
    copies[2].wait()
    spread_rows(smooth_ref, smooth_spread, smooth_copies(smooth_width))

    for group in range(rows // quad):
        weights, values = [], []
        for member in range(quad):
            row = perm_ref[quad * group + member]
            weights.append(spread_row(smooth_spread, row, half, 0, half))
            straight = spread_row(right_spread, row, len(copied), 0, SUB)
            crossed = spread_row(right_spread, row, len(copied), SUB // 2, SUB)
            values += [jnp.where(lower, straight, 0.0), jnp.where(lower, 0.0, crossed)]
        products = lax.dot_general(
            jnp.concatenate(values, axis=0).astype(jnp.bfloat16),
            jnp.concatenate(weights, axis=0).astype(jnp.bfloat16),
            TRANSPOSED,
            preferred_element_type=jnp.float32,
        )
        own = products[: 2 * SUB]
        for member in range(1, quad):
            own = jnp.where(
                lanes // half == member, products[2 * SUB * member : 2 * SUB * (member + 1)], own
            )
        collected[pl.ds(group * SUB, SUB), :LANES] = own[:SUB]
        collected[pl.ds(group * SUB, SUB), LANES:] = own[SUB:]
    ordered = lax.dot_general(
        collected[...].astype(jnp.bfloat16), order, PLAIN, preferred_element_type=jnp.float32
    ).astype(jnp.bfloat16)
    for group in range(rows // quad):
        for pair in range(quad // 2):
            xb_ref[group * (quad // 2) + pair] = ordered[
                group * SUB : (group + 1) * SUB, pair * LANES : (pair + 1) * LANES
            ]


def find_tiles(groups, members, pairs, cols, mask, dest, own_row, own_group):
    slots = groups * members * CAP
    rank = cols % CAP
    source = (cols % slots) // CAP
    position = ((dest // members) * members + cols // slots) * CAP + rank
    return place_tiles(groups, members, pairs, source, position, mask, own_row, own_group)


def place_tiles(groups, members, pairs, source, position, mask, own_row, own_group):
    relative_row = (source % members) ^ own_row
    relative_group = (source // members) ^ own_group
    piece = (relative_row % 2) * groups + relative_group
    within = jnp.zeros_like(piece)
    for order, bit in enumerate(row_bits(members)):
        within = within + ((relative_row // bit) % 2) * (1 << order)
    tile = (piece * (members // 2) + within) * pairs + position // 2
    swap = (position + lax.broadcasted_iota(jnp.int32, position.shape, 0)) % 2
    return jnp.where(mask != 0, tile * 2 + swap, 2 * groups * members * pairs)


def in_hbm(value):
    return pltpu.with_memory_space_constraint(value, pltpu.HBM)


def row_bits(members):
    return [1 << bit for bit in range(members.bit_length() - 2, 0, -1)]


def prepare(
    full, groups, members, perm_ref, rounded_ref, cols_hbm, mask_hbm, dest_hbm, smooth_hbm, right_hbm, blocks_hbm,
    own_ref, index_ref, x_ref, rp_ref, sbd_ref, blocks_ref,
    cols_ref, mask_ref, dest_ref, smooth_ref, right_ref, smooth_spread, right_spread, widened, sems,
):
    moves = [
        (cols_hbm, cols_ref), (mask_hbm, mask_ref), (dest_hbm, dest_ref),
        (right_hbm, right_ref), (smooth_hbm, smooth_ref), (blocks_hbm, blocks_ref),
    ]
    copies = [pltpu.make_async_copy(*move, sems.at[number]) for number, move in enumerate(moves)]
    for copy in copies:
        copy.start()
    rows, smooth_width = smooth_ref.shape
    block = LANES // 2
    half = smooth_width // LANES
    pairs = rows // 2
    lower = lax.broadcasted_iota(jnp.int32, (SUB, LANES), 1) < block
    low_half = lax.broadcasted_iota(jnp.int32, (half, LANES), 1) < block
    own_ref[...] = rounded_ref[...]
    for copy in copies[:3]:
        copy.wait()
    if full:
        index_ref[...] = find_tiles(
            groups, members, pairs, cols_ref[...], mask_ref[...], dest_ref[...],
            lax.axis_index("row"), lax.axis_index("grp"),
        )
    else:
        index_ref[...] = cols_ref[...]
    copies[3].wait()
    copied = right_copies(right_ref.shape[1])
    spread_rows(right_ref, right_spread, copied)
    copies[4].wait()
    spread_rows(smooth_ref, smooth_spread, smooth_copies(smooth_width))
    for pair in range(pairs):
        low, high = perm_ref[2 * pair], perm_ref[2 * pair + 1]
        rp_ref[pair] = jnp.where(
            lower,
            spread_row(right_spread, low, len(copied), 0, SUB),
            spread_row(right_spread, high, len(copied), SUB // 2, SUB),
        ).astype(jnp.bfloat16)
        base = pair * LANES
        for number, row in enumerate((low, high)):
            straight = spread_row(smooth_spread, row, half, 0, half)
            turned = pltpu.roll(straight, block, 1)
            first, second = (straight, turned) if number == 0 else (turned, straight)
            keep = low_half if number == 0 else jnp.logical_not(low_half)
            widened[pl.ds(base + number * block, half, stride=2), :] = jnp.where(keep, first, 0.0)
            widened[pl.ds(base + number * block + 1, half, stride=2), :] = jnp.where(keep, second, 0.0)
    for pair in range(pairs):
        sbd_ref[pair] = widened[pl.ds(pair * LANES, LANES), :].astype(jnp.bfloat16)
    for pair in range(pairs):
        x_ref[pair] = lax.dot_general(
            rp_ref[pair], sbd_ref[pair], TRANSPOSED, preferred_element_type=jnp.float32
        )
    copies[5].wait()


def later_sweep(piece_count, with_rounded, *refs):
    perm_ref, index_ref = refs[:2]
    pieces = refs[2 : 2 + piece_count]
    blocks, sbd_ref, rp_ref, x_ref = refs[2 + piece_count : 6 + piece_count]
    refs = refs[6 + piece_count :]
    out_ref = refs[0]
    rounded_ref = refs[1] if with_rounded else None
    tiles, defects, tile_sem = refs[2 if with_rounded else 1 :]
    pairs = x_ref.shape[0]
    _, block, width = blocks.shape
    bands = width // block
    piece_tiles = pieces[0].shape[0]

    tile_copies = [
        pltpu.make_async_copy(piece, tiles.at[pl.ds(number * piece_tiles, piece_tiles)], tile_sem.at[number])
        for number, piece in enumerate(pieces)
    ]
    for copy in tile_copies:
        copy.start()
    tiles[piece_count * piece_tiles] = jnp.zeros((NRHS, LANES), jnp.bfloat16)
    for copy in tile_copies:
        copy.wait()

    lower = lax.broadcasted_iota(jnp.int32, (NRHS, LANES), 1) < block

    def fetch(row, band):
        entry = index_ref[band, row]
        tile = tiles[lax.shift_right_logical(entry, 1)].astype(jnp.float32)
        return pltpu.roll(tile, (entry & 1) * block, 1)

    def values(row):
        return [
            jnp.where(lower, fetch(row, 2 * half), fetch(row, 2 * half + 1)) for half in range(bands // 2)
        ]

    for pair in range(pairs):
        low, high = perm_ref[2 * pair], perm_ref[2 * pair + 1]
        gathered = jnp.concatenate(
            [
                jnp.concatenate(values(low), axis=1),
                jnp.concatenate(values(high), axis=1),
            ],
            axis=0,
        ).astype(jnp.bfloat16)
        weights = jnp.concatenate([blocks[low], blocks[high]], axis=0)
        applied = lax.dot_general(gathered, weights, TRANSPOSED, preferred_element_type=jnp.float32)
        image = jnp.where(lower, applied[:NRHS], applied[NRHS:])
        defects[pair] = (rp_ref[pair].astype(jnp.float32) - image).astype(jnp.bfloat16)

    for pair in range(pairs):
        x = x_ref[pair] + lax.dot_general(
            defects[pair], sbd_ref[pair], TRANSPOSED, preferred_element_type=jnp.float32
        )
        out_ref[pair] = x
        if with_rounded:
            rounded_ref[pair] = x.astype(jnp.bfloat16)


def local(coarse_blocks, smoother, residual, dest, band_cols, band_mask):
    groups = lax.axis_size("grp")
    members = lax.axis_size("row")
    devices = groups * members
    rows, block, width = coarse_blocks.shape
    bands = band_cols.shape[1]
    pairs = rows // 2
    full = rows == devices * CAP
    smem = pl.BlockSpec(memory_space=pltpu.SMEM)
    vmem = pl.BlockSpec(memory_space=pltpu.VMEM)
    hbm = pl.BlockSpec(memory_space=pltpu.HBM)
    anywhere = pl.BlockSpec(memory_space=pl.ANY)
    tile_shape = (pairs, NRHS, LANES)
    params = pltpu.CompilerParams(vmem_limit_bytes=VMEM_LIMIT)

    smooth_width, right_width = smoother.shape[1], residual.shape[1]
    smooth_rows = rows * len(smooth_copies(smooth_width))
    right_rows = rows * len(right_copies(right_width))
    perm, starts, rounded = pl.pallas_call(
        functools.partial(first_sweep, full),
        out_shape=(
            jax.ShapeDtypeStruct((rows,), jnp.int32),
            jax.ShapeDtypeStruct((devices,), jnp.int32),
            jax.ShapeDtypeStruct(tile_shape, jnp.bfloat16),
        ),
        in_specs=[hbm] * 3,
        out_specs=(smem, smem, vmem),
        scratch_shapes=[
            pltpu.SMEM((rows,), jnp.int32),
            pltpu.SMEM((devices,), jnp.int32),
            pltpu.VMEM(smoother.shape, jnp.bfloat16),
            pltpu.VMEM(residual.shape, jnp.bfloat16),
            pltpu.VMEM((smooth_rows, LANES), jnp.float32),
            pltpu.VMEM((right_rows, LANES), jnp.float32),
            pltpu.VMEM((pairs * SUB // 2, 2 * LANES), jnp.float32),
            pltpu.SemaphoreType.DMA((3,)),
        ],
        compiler_params=params,
        name="first_sweep",
    )(in_hbm(dest.reshape(rows)), in_hbm(smoother), in_hbm(residual))
    cols, mask = band_cols.T, band_mask.T
    if not full:
        slots = devices * CAP
        table = lax.all_gather(starts, ("grp", "row"), axis=0, tiled=True)
        source = (cols % slots) // CAP
        owner = (dest.T // members) * members + cols // slots
        position = jnp.take(table, source * devices + owner, mode="clip") + cols % CAP
        cols = place_tiles(
            groups, members, pairs, source, position, mask, lax.axis_index("row"), lax.axis_index("grp")
        )
    own, index, x, right, smooth, blocks = pl.pallas_call(
        functools.partial(prepare, full, groups, members),
        out_shape=(
            jax.ShapeDtypeStruct(tile_shape, jnp.bfloat16),
            jax.ShapeDtypeStruct((bands, rows), jnp.int32),
            jax.ShapeDtypeStruct(tile_shape, jnp.float32),
            jax.ShapeDtypeStruct(tile_shape, jnp.bfloat16),
            jax.ShapeDtypeStruct((pairs, 2 * block, 2 * block), jnp.bfloat16),
            jax.ShapeDtypeStruct(coarse_blocks.shape, jnp.bfloat16),
        ),
        in_specs=[smem, vmem] + [hbm] * 6,
        out_specs=(vmem,) * 6,
        scratch_shapes=[
            pltpu.VMEM((bands, rows), jnp.int32),
            pltpu.VMEM((bands, rows), jnp.int32),
            pltpu.VMEM((1, rows), jnp.int32),
            pltpu.VMEM(smoother.shape, jnp.bfloat16),
            pltpu.VMEM(residual.shape, jnp.bfloat16),
            pltpu.VMEM((smooth_rows, LANES), jnp.float32),
            pltpu.VMEM((right_rows, LANES), jnp.float32),
            pltpu.VMEM((pairs * LANES, LANES), jnp.float32),
            pltpu.SemaphoreType.DMA((6,)),
        ],
        compiler_params=params,
        cost_estimate=pl.CostEstimate(flops=1 << 26, bytes_accessed=10 << 20, transcendentals=0),
        name="prepare",
    )(
        perm, rounded, in_hbm(cols), in_hbm(mask), in_hbm(dest.T),
        in_hbm(smoother), in_hbm(residual), in_hbm(coarse_blocks),
    )

    def exchange(value, axis, size, distance):
        return lax.ppermute(value, axis, [(place, place ^ distance) for place in range(size)])

    def everywhere(value, own):
        for bit in row_bits(members):
            value = own = jnp.concatenate([own, exchange(value, "row", members, bit)], axis=0)
        near = [value] + [exchange(value, "grp", groups, distance) for distance in range(1, groups)]
        return near + [exchange(part, "row", members, 1) for part in near]

    def sweep(x, rounded, own, last):
        pieces = everywhere(rounded, own)
        outs = [jax.ShapeDtypeStruct(tile_shape, jnp.float32)]
        if not last:
            outs.append(jax.ShapeDtypeStruct(tile_shape, jnp.bfloat16))
        return pl.pallas_call(
            functools.partial(later_sweep, len(pieces), not last),
            out_shape=tuple(outs),
            in_specs=[smem, smem] + [anywhere] * len(pieces) + [vmem] * 4,
            out_specs=tuple([vmem] * len(outs)),
            scratch_shapes=[
                pltpu.VMEM((devices * pairs + 1, NRHS, LANES), jnp.bfloat16),
                pltpu.VMEM(tile_shape, jnp.bfloat16),
                pltpu.SemaphoreType.DMA((len(pieces),)),
            ],
            compiler_params=params,
            name="later_sweep",
        )(perm, index, *pieces, blocks, smooth, right, x)

    x, rounded = sweep(x, rounded, own, False)
    (x,) = sweep(x, rounded, rounded, True)

    if not full:
        flat = x.reshape(pairs, 2, NRHS // 2, 2, block).transpose(0, 3, 2, 1, 4).reshape(rows, NRHS * block)
        following = jnp.concatenate([starts[1:], jnp.full((1,), rows, jnp.int32)])
        slots = devices * CAP
        wanted = starts[:, None] + jnp.arange(CAP, dtype=jnp.int32)[None, :]
        live = wanted < following[:, None]
        flat = jnp.where(
            live.reshape(slots, 1), jnp.take(flat, wanted.reshape(slots), axis=0, mode="clip"), 0.0
        )
        x = flat.reshape(devices, CAP, NRHS // 2, 2, block).transpose(0, 3, 2, 1, 4)
        x = x.reshape(devices, NRHS, CAP * block)
    got = lax.all_to_all(x, ("grp", "row"), split_axis=0, concat_axis=0, tiled=True)
    got = got.reshape(devices, 2, NRHS // 2, CAP, block).transpose(0, 3, 2, 1, 4)
    return got.reshape(devices * CAP, NRHS * block)


def solution(mesh):
    in_specs = (
        P(("grp", "row"), None, None),
        P(("grp", "row"), None),
        P(("grp", "row"), None),
        P(("grp", "row"), None),
        P(("grp", "row"), None),
        P(("grp", "row"), None),
    )
    out_specs = P(("grp", "row"), None)
    return jax.shard_map(local, mesh=mesh, in_specs=in_specs, out_specs=out_specs, check_vma=False)
```

```python
import functools

import jax
import jax.numpy as jnp
from jax import lax
from jax.experimental import pallas as pl
from jax.experimental.pallas import tpu as pltpu
from jax.sharding import PartitionSpec as P

NRHS = 8
CAP = 2
LANES = 128
VMEM_LIMIT = 32 * 1024 * 1024

TRANSPOSED = (((1,), (1,)), ((), ()))
PLAIN = (((1,), (0,)), ((), ()))
SUB = 8


def spread_rows(source_ref, spread_ref, copies):
    rows, width = source_ref.shape
    tiles = width // LANES
    for top in range(rows // SUB):
        values = source_ref[top * SUB : (top + 1) * SUB, :].astype(jnp.float32)
        for place, (tile, turned) in enumerate(copies):
            piece = values[:, tile * LANES : (tile + 1) * LANES]
            if turned:
                piece = pltpu.roll(piece, LANES // 2, 1)
            spread_ref[pl.ds((top * len(copies) + place) * SUB, SUB), :] = piece


def spread_row(spread_ref, row, tiles, first, count):
    start = (row // SUB) * (tiles * SUB) + first * SUB + row % SUB
    return spread_ref[pl.ds(start, count, stride=SUB), :]


def smooth_copies(width):
    return [(tile, False) for tile in range(width // LANES)]


def right_copies(width):
    plain = [(tile, False) for tile in range(width // LANES)]
    turned = [(tile, True) for tile in range(width // LANES)]
    return plain + turned + plain


def sort_rows(full, dest_ref, perm_ref, starts_ref, count):
    rows = dest_ref.shape[0]
    owners = starts_ref.shape[0]
    if full:
        for owner in range(owners):
            count[owner] = owner * CAP
            starts_ref[owner] = owner * CAP
    else:

        def clear(owner, carry):
            count[owner] = 0
            return carry

        lax.fori_loop(0, owners, clear, 0)

        def tally(row, carry):
            count[dest_ref[row]] = count[dest_ref[row]] + 1
            return carry

        lax.fori_loop(0, rows, tally, 0)

        def start(owner, total):
            following = total + count[owner]
            starts_ref[owner] = total
            count[owner] = total
            return following

        lax.fori_loop(0, owners, start, jnp.int32(0))
    for row in range(rows):
        owner = dest_ref[row]
        position = count[owner]
        count[owner] = position + 1
        perm_ref[position] = row


def first_sweep(
    full, dest_hbm, smooth_hbm, right_hbm, perm_ref, starts_ref, xb_ref,
    dest_ref, count, smooth_ref, right_ref, smooth_spread, right_spread, collected, sems,
):
    copies = [
        pltpu.make_async_copy(dest_hbm, dest_ref, sems.at[0]),
        pltpu.make_async_copy(right_hbm, right_ref, sems.at[1]),
        pltpu.make_async_copy(smooth_hbm, smooth_ref, sems.at[2]),
    ]
    for copy in copies:
        copy.start()
    rows, smooth_width = smooth_ref.shape
    block = LANES // 2
    half = smooth_width // LANES
    quad = LANES // half
    lanes = lax.broadcasted_iota(jnp.int32, (2 * SUB, LANES), 1)
    lower = lanes[:SUB] < block
    width = quad * block
    held = lax.broadcasted_iota(jnp.int32, (width, width), 0)
    wanted = lax.broadcasted_iota(jnp.int32, (width, width), 1)
    placed = ((held % LANES) // half) * block + 2 * (held % half) + held // LANES
    order = jnp.where(placed == wanted, 1.0, 0.0).astype(jnp.bfloat16)

    copies[0].wait()
    sort_rows(full, dest_ref, perm_ref, starts_ref, count)
    copies[1].wait()
    copied = right_copies(right_ref.shape[1])
    spread_rows(right_ref, right_spread, copied)
    copies[2].wait()
    spread_rows(smooth_ref, smooth_spread, smooth_copies(smooth_width))

    for group in range(rows // quad):
        weights, values = [], []
        for member in range(quad):
            row = perm_ref[quad * group + member]
            weights.append(spread_row(smooth_spread, row, half, 0, half))
            straight = spread_row(right_spread, row, len(copied), 0, SUB)
            crossed = spread_row(right_spread, row, len(copied), SUB // 2, SUB)
            values += [jnp.where(lower, straight, 0.0), jnp.where(lower, 0.0, crossed)]
        products = lax.dot_general(
            jnp.concatenate(values, axis=0).astype(jnp.bfloat16),
            jnp.concatenate(weights, axis=0).astype(jnp.bfloat16),
            TRANSPOSED,
            preferred_element_type=jnp.float32,
        )
        own = products[: 2 * SUB]
        for member in range(1, quad):
            own = jnp.where(
                lanes // half == member, products[2 * SUB * member : 2 * SUB * (member + 1)], own
            )
        collected[pl.ds(group * SUB, SUB), :LANES] = own[:SUB]
        collected[pl.ds(group * SUB, SUB), LANES:] = own[SUB:]
    ordered = lax.dot_general(
        collected[...].astype(jnp.bfloat16), order, PLAIN, preferred_element_type=jnp.float32
    ).astype(jnp.bfloat16)
    for group in range(rows // quad):
        for pair in range(quad // 2):
            xb_ref[group * (quad // 2) + pair] = ordered[
                group * SUB : (group + 1) * SUB, pair * LANES : (pair + 1) * LANES
            ]


def find_tiles(groups, members, pairs, cols, mask, dest, own_row, own_group):
    slots = groups * members * CAP
    rank = cols % CAP
    source = (cols % slots) // CAP
    position = ((dest // members) * members + cols // slots) * CAP + rank
    return place_tiles(groups, members, pairs, source, position, mask, own_row, own_group)


def place_tiles(groups, members, pairs, source, position, mask, own_row, own_group):
    relative_row = (source % members) ^ own_row
    relative_group = (source // members) ^ own_group
    piece = (relative_row % 2) * groups + relative_group
    within = jnp.zeros_like(piece)
    for parity in range(2):
        for order, bit in enumerate(row_bits(members, parity)):
            within = within + jnp.where(source % 2 == parity, ((relative_row // bit) % 2) * (1 << order), 0)
    tile = (piece * (members // 2) + within) * pairs + position // 2
    swap = (position + lax.broadcasted_iota(jnp.int32, position.shape, 0)) % 2
    return jnp.where(mask != 0, tile * 2 + swap, 2 * groups * members * pairs)


def row_bits(members, parity):
    bits = [1 << bit for bit in range(members.bit_length() - 2, 0, -1)]
    return bits[::-1] if parity else bits


def in_hbm(value):
    return pltpu.with_memory_space_constraint(value, pltpu.HBM)


def prepare(
    full, groups, members, perm_ref, rounded_ref, cols_hbm, mask_hbm, dest_hbm, smooth_hbm, right_hbm, blocks_hbm,
    own_ref, index_ref, x_ref, rp_ref, sbd_ref, blocks_ref,
    cols_ref, mask_ref, dest_ref, smooth_ref, right_ref, smooth_spread, right_spread, widened, sems,
):
    moves = [
        (cols_hbm, cols_ref), (mask_hbm, mask_ref), (dest_hbm, dest_ref),
        (right_hbm, right_ref), (smooth_hbm, smooth_ref), (blocks_hbm, blocks_ref),
    ]
    copies = [pltpu.make_async_copy(*move, sems.at[number]) for number, move in enumerate(moves)]
    for copy in copies:
        copy.start()
    rows, smooth_width = smooth_ref.shape
    block = LANES // 2
    half = smooth_width // LANES
    pairs = rows // 2
    lower = lax.broadcasted_iota(jnp.int32, (SUB, LANES), 1) < block
    low_half = lax.broadcasted_iota(jnp.int32, (half, LANES), 1) < block
    own_ref[...] = rounded_ref[...]
    for copy in copies[:3]:
        copy.wait()
    if full:
        index_ref[...] = find_tiles(
            groups, members, pairs, cols_ref[...], mask_ref[...], dest_ref[...],
            lax.axis_index("row"), lax.axis_index("grp"),
        )
    else:
        index_ref[...] = cols_ref[...]
    copies[3].wait()
    copied = right_copies(right_ref.shape[1])
    spread_rows(right_ref, right_spread, copied)
    copies[4].wait()
    spread_rows(smooth_ref, smooth_spread, smooth_copies(smooth_width))
    for pair in range(pairs):
        low, high = perm_ref[2 * pair], perm_ref[2 * pair + 1]
        rp_ref[pair] = jnp.where(
            lower,
            spread_row(right_spread, low, len(copied), 0, SUB),
            spread_row(right_spread, high, len(copied), SUB // 2, SUB),
        ).astype(jnp.bfloat16)
        base = pair * LANES
        for number, row in enumerate((low, high)):
            straight = spread_row(smooth_spread, row, half, 0, half)
            turned = pltpu.roll(straight, block, 1)
            first, second = (straight, turned) if number == 0 else (turned, straight)
            keep = low_half if number == 0 else jnp.logical_not(low_half)
            widened[pl.ds(base + number * block, half, stride=2), :] = jnp.where(keep, first, 0.0)
            widened[pl.ds(base + number * block + 1, half, stride=2), :] = jnp.where(keep, second, 0.0)
    for pair in range(pairs):
        sbd_ref[pair] = widened[pl.ds(pair * LANES, LANES), :].astype(jnp.bfloat16)
    for pair in range(pairs):
        x_ref[pair] = lax.dot_general(
            rp_ref[pair], sbd_ref[pair], TRANSPOSED, preferred_element_type=jnp.float32
        )
    copies[5].wait()


def later_sweep(piece_count, with_rounded, *refs):
    perm_ref, index_ref = refs[:2]
    pieces = refs[2 : 2 + piece_count]
    blocks, sbd_ref, rp_ref, x_ref = refs[2 + piece_count : 6 + piece_count]
    refs = refs[6 + piece_count :]
    out_ref = refs[0]
    rounded_ref = refs[1] if with_rounded else None
    tiles, defects = refs[2 if with_rounded else 1 :]
    pairs = x_ref.shape[0]
    _, block, width = blocks.shape
    bands = width // block

    start = 0
    for piece in pieces:
        size = piece.shape[0]
        tiles[pl.ds(start, size)] = piece[...]
        start += size
    tiles[start] = jnp.zeros((NRHS, LANES), jnp.bfloat16)

    lower = lax.broadcasted_iota(jnp.int32, (NRHS, LANES), 1) < block

    first_half = lax.broadcasted_iota(jnp.int32, (NRHS, LANES), 0) < NRHS // 2

    def fetch(row, band):
        entry = index_ref[band, row]
        tile = tiles[lax.shift_right_logical(entry, 1)].astype(jnp.float32)
        return pltpu.roll(tile, (entry & 1) * block, 1)

    def values(row):
        return [
            jnp.where(lower, fetch(row, 2 * half), fetch(row, 2 * half + 1)) for half in range(bands // 2)
        ]

    for pair in range(pairs):
        low, high = perm_ref[2 * pair], perm_ref[2 * pair + 1]
        gathered = jnp.concatenate(
            [
                jnp.concatenate(values(low), axis=1),
                jnp.concatenate(values(high), axis=1),
            ],
            axis=0,
        ).astype(jnp.bfloat16)
        weights = jnp.concatenate([blocks[low], blocks[high]], axis=0)
        applied = lax.dot_general(gathered, weights, TRANSPOSED, preferred_element_type=jnp.float32)
        image = jnp.where(lower, applied[:NRHS], applied[NRHS:])
        defects[pair] = (rp_ref[pair].astype(jnp.float32) - image).astype(jnp.bfloat16)

    for pair in range(pairs):
        x = x_ref[pair] + lax.dot_general(
            defects[pair], sbd_ref[pair], TRANSPOSED, preferred_element_type=jnp.float32
        )
        if with_rounded:
            out_ref[pair] = x
            rounded_ref[pair] = x.astype(jnp.bfloat16)
        else:
            crossed = pltpu.roll(pltpu.roll(x, block, 1), NRHS // 2, 0)
            out_ref[pair] = jnp.where(lower == first_half, x, crossed)


def lay_out(got_ref, out_ref):
    rows, width = out_ref.shape
    tiles = width // LANES
    for tile in range(tiles):
        out_ref[:, tile * LANES : (tile + 1) * LANES] = got_ref[pl.ds(tile, rows, stride=tiles), :]


def local(coarse_blocks, smoother, residual, dest, band_cols, band_mask):
    groups = lax.axis_size("grp")
    members = lax.axis_size("row")
    devices = groups * members
    rows, block, width = coarse_blocks.shape
    bands = band_cols.shape[1]
    pairs = rows // 2
    full = rows == devices * CAP
    smem = pl.BlockSpec(memory_space=pltpu.SMEM)
    vmem = pl.BlockSpec(memory_space=pltpu.VMEM)
    hbm = pl.BlockSpec(memory_space=pltpu.HBM)
    tile_shape = (pairs, NRHS, LANES)
    params = pltpu.CompilerParams(vmem_limit_bytes=VMEM_LIMIT)

    smooth_width, right_width = smoother.shape[1], residual.shape[1]
    smooth_rows = rows * len(smooth_copies(smooth_width))
    right_rows = rows * len(right_copies(right_width))
    perm, starts, rounded = pl.pallas_call(
        functools.partial(first_sweep, full),
        out_shape=(
            jax.ShapeDtypeStruct((rows,), jnp.int32),
            jax.ShapeDtypeStruct((devices,), jnp.int32),
            jax.ShapeDtypeStruct(tile_shape, jnp.bfloat16),
        ),
        in_specs=[hbm] * 3,
        out_specs=(smem, smem, vmem),
        scratch_shapes=[
            pltpu.SMEM((rows,), jnp.int32),
            pltpu.SMEM((devices,), jnp.int32),
            pltpu.VMEM(smoother.shape, jnp.bfloat16),
            pltpu.VMEM(residual.shape, jnp.bfloat16),
            pltpu.VMEM((smooth_rows, LANES), jnp.float32),
            pltpu.VMEM((right_rows, LANES), jnp.float32),
            pltpu.VMEM((pairs * SUB // 2, 2 * LANES), jnp.float32),
            pltpu.SemaphoreType.DMA((3,)),
        ],
        compiler_params=params,
        name="first_sweep",
    )(in_hbm(dest.reshape(rows)), in_hbm(smoother), in_hbm(residual))
    cols, mask = band_cols.T, band_mask.T
    if not full:
        slots = devices * CAP
        table = lax.all_gather(starts, ("grp", "row"), axis=0, tiled=True)
        source = (cols % slots) // CAP
        owner = (dest.T // members) * members + cols // slots
        position = jnp.take(table, source * devices + owner, mode="clip") + cols % CAP
        cols = place_tiles(
            groups, members, pairs, source, position, mask, lax.axis_index("row"), lax.axis_index("grp")
        )
    own, index, x, right, smooth, blocks = pl.pallas_call(
        functools.partial(prepare, full, groups, members),
        out_shape=(
            jax.ShapeDtypeStruct(tile_shape, jnp.bfloat16),
            jax.ShapeDtypeStruct((bands, rows), jnp.int32),
            jax.ShapeDtypeStruct(tile_shape, jnp.float32),
            jax.ShapeDtypeStruct(tile_shape, jnp.bfloat16),
            jax.ShapeDtypeStruct((pairs, 2 * block, 2 * block), jnp.bfloat16),
            jax.ShapeDtypeStruct(coarse_blocks.shape, jnp.bfloat16),
        ),
        in_specs=[smem, vmem] + [hbm] * 6,
        out_specs=(vmem,) * 6,
        scratch_shapes=[
            pltpu.VMEM((bands, rows), jnp.int32),
            pltpu.VMEM((bands, rows), jnp.int32),
            pltpu.VMEM((1, rows), jnp.int32),
            pltpu.VMEM(smoother.shape, jnp.bfloat16),
            pltpu.VMEM(residual.shape, jnp.bfloat16),
            pltpu.VMEM((smooth_rows, LANES), jnp.float32),
            pltpu.VMEM((right_rows, LANES), jnp.float32),
            pltpu.VMEM((pairs * LANES, LANES), jnp.float32),
            pltpu.SemaphoreType.DMA((6,)),
        ],
        compiler_params=params,
        cost_estimate=pl.CostEstimate(flops=1 << 26, bytes_accessed=10 << 20, transcendentals=0),
        name="prepare",
    )(
        perm, rounded, in_hbm(cols), in_hbm(mask), in_hbm(dest.T),
        in_hbm(smoother), in_hbm(residual), in_hbm(coarse_blocks),
    )

    def exchange_row(value, distances):
        return lax.ppermute(value, "row", [(place, place ^ distances[place % 2]) for place in range(members)])

    def everywhere(value, own):
        for distances in zip(row_bits(members, 0), row_bits(members, 1)):
            value = own = jnp.concatenate([own, exchange_row(value, distances)], axis=0)
        near = [own] + [
            lax.ppermute(own, "grp", [(place, place ^ distance) for place in range(groups)])
            for distance in range(1, groups)
        ]
        return near + [exchange_row(part, (1, 1)) for part in near]

    def sweep(x, rounded, own, last):
        pieces = everywhere(rounded, own)
        outs = [jax.ShapeDtypeStruct(tile_shape, jnp.float32)]
        if not last:
            outs.append(jax.ShapeDtypeStruct(tile_shape, jnp.bfloat16))
        return pl.pallas_call(
            functools.partial(later_sweep, len(pieces), not last),
            out_shape=tuple(outs),
            in_specs=[smem, smem] + [vmem] * (len(pieces) + 4),
            out_specs=tuple([vmem] * len(outs)),
            scratch_shapes=[
                pltpu.VMEM((devices * pairs + 1, NRHS, LANES), jnp.bfloat16),
                pltpu.VMEM(tile_shape, jnp.bfloat16),
            ],
            compiler_params=params,
            name="later_sweep",
        )(perm, index, *pieces, blocks, smooth, right, x)

    x, rounded = sweep(x, rounded, own, False)
    (x,) = sweep(x, rounded, rounded, True)

    if not full:
        flat = x.reshape(rows, NRHS * block)
        following = jnp.concatenate([starts[1:], jnp.full((1,), rows, jnp.int32)])
        slots = devices * CAP
        wanted = starts[:, None] + jnp.arange(CAP, dtype=jnp.int32)[None, :]
        live = wanted < following[:, None]
        flat = jnp.where(
            live.reshape(slots, 1), jnp.take(flat, wanted.reshape(slots), axis=0, mode="clip"), 0.0
        )
        x = flat.reshape(devices, NRHS, LANES)
    got = lax.all_to_all(x, ("grp", "row"), split_axis=0, concat_axis=0, tiled=True)
    return pl.pallas_call(
        lay_out,
        out_shape=jax.ShapeDtypeStruct((devices * CAP, NRHS * block), jnp.float32),
        in_specs=[vmem],
        out_specs=vmem,
        compiler_params=params,
        name="lay_out",
    )(got.reshape(devices * NRHS, LANES))


def solution(mesh):
    in_specs = (
        P(("grp", "row"), None, None),
        P(("grp", "row"), None),
        P(("grp", "row"), None),
        P(("grp", "row"), None),
        P(("grp", "row"), None),
        P(("grp", "row"), None),
    )
    out_specs = P(("grp", "row"), None)
    return jax.shard_map(local, mesh=mesh, in_specs=in_specs, out_specs=out_specs, check_vma=False)
```

```python
import functools

import jax
import jax.numpy as jnp
from jax import lax
from jax.experimental import pallas as pl
from jax.experimental.pallas import tpu as pltpu
from jax.sharding import PartitionSpec as P

NRHS = 8
CAP = 2
LANES = 128
VMEM_LIMIT = 32 * 1024 * 1024

TRANSPOSED = (((1,), (1,)), ((), ()))
PLAIN = (((1,), (0,)), ((), ()))
SUB = 8


def spread_rows(source_ref, spread_ref, copies):
    rows, width = source_ref.shape
    tiles = width // LANES
    for top in range(rows // SUB):
        values = source_ref[top * SUB : (top + 1) * SUB, :].astype(jnp.float32)
        for place, (tile, turned) in enumerate(copies):
            piece = values[:, tile * LANES : (tile + 1) * LANES]
            if turned:
                piece = pltpu.roll(piece, LANES // 2, 1)
            spread_ref[pl.ds((top * len(copies) + place) * SUB, SUB), :] = piece


def spread_row(spread_ref, row, tiles, first, count):
    start = (row // SUB) * (tiles * SUB) + first * SUB + row % SUB
    return spread_ref[pl.ds(start, count, stride=SUB), :]


def smooth_copies(width):
    return [(tile, False) for tile in range(width // LANES)]


def right_copies(width):
    plain = [(tile, False) for tile in range(width // LANES)]
    turned = [(tile, True) for tile in range(width // LANES)]
    return plain + turned + plain


def sort_rows(full, dest_ref, perm_ref, starts_ref, count):
    rows = dest_ref.shape[0]
    owners = starts_ref.shape[0]
    if full:
        for owner in range(owners):
            count[owner] = owner * CAP
            starts_ref[owner] = owner * CAP
    else:

        def clear(owner, carry):
            count[owner] = 0
            return carry

        lax.fori_loop(0, owners, clear, 0)

        def tally(row, carry):
            count[dest_ref[row]] = count[dest_ref[row]] + 1
            return carry

        lax.fori_loop(0, rows, tally, 0)

        def start(owner, total):
            following = total + count[owner]
            starts_ref[owner] = total
            count[owner] = total
            return following

        lax.fori_loop(0, owners, start, jnp.int32(0))
    for row in range(rows):
        owner = dest_ref[row]
        position = count[owner]
        count[owner] = position + 1
        perm_ref[position] = row


def first_sweep(
    full, dest_hbm, smooth_hbm, right_hbm, perm_ref, starts_ref, xb_ref,
    dest_ref, count, smooth_ref, right_ref, smooth_spread, right_spread, collected, sems,
):
    copies = [
        pltpu.make_async_copy(dest_hbm, dest_ref, sems.at[0]),
        pltpu.make_async_copy(right_hbm, right_ref, sems.at[1]),
        pltpu.make_async_copy(smooth_hbm, smooth_ref, sems.at[2]),
    ]
    for copy in copies:
        copy.start()
    rows, smooth_width = smooth_ref.shape
    block = LANES // 2
    half = smooth_width // LANES
    quad = LANES // half
    lanes = lax.broadcasted_iota(jnp.int32, (2 * SUB, LANES), 1)
    lower = lanes[:SUB] < block
    width = quad * block
    held = lax.broadcasted_iota(jnp.int32, (width, width), 0)
    wanted = lax.broadcasted_iota(jnp.int32, (width, width), 1)
    placed = ((held % LANES) // half) * block + 2 * (held % half) + held // LANES
    order = jnp.where(placed == wanted, 1.0, 0.0).astype(jnp.bfloat16)

    copies[0].wait()
    sort_rows(full, dest_ref, perm_ref, starts_ref, count)
    copies[1].wait()
    copied = right_copies(right_ref.shape[1])
    spread_rows(right_ref, right_spread, copied)
    copies[2].wait()
    spread_rows(smooth_ref, smooth_spread, smooth_copies(smooth_width))

    for group in range(rows // quad):
        weights, values = [], []
        for member in range(quad):
            row = perm_ref[quad * group + member]
            weights.append(spread_row(smooth_spread, row, half, 0, half))
            straight = spread_row(right_spread, row, len(copied), 0, SUB)
            crossed = spread_row(right_spread, row, len(copied), SUB // 2, SUB)
            values += [jnp.where(lower, straight, 0.0), jnp.where(lower, 0.0, crossed)]
        products = lax.dot_general(
            jnp.concatenate(values, axis=0).astype(jnp.bfloat16),
            jnp.concatenate(weights, axis=0).astype(jnp.bfloat16),
            TRANSPOSED,
            preferred_element_type=jnp.float32,
        )
        own = products[: 2 * SUB]
        for member in range(1, quad):
            own = jnp.where(
                lanes // half == member, products[2 * SUB * member : 2 * SUB * (member + 1)], own
            )
        collected[pl.ds(group * SUB, SUB), :LANES] = own[:SUB]
        collected[pl.ds(group * SUB, SUB), LANES:] = own[SUB:]
    ordered = lax.dot_general(
        collected[...].astype(jnp.bfloat16), order, PLAIN, preferred_element_type=jnp.float32
    ).astype(jnp.bfloat16)
    for group in range(rows // quad):
        for pair in range(quad // 2):
            xb_ref[group * (quad // 2) + pair] = ordered[
                group * SUB : (group + 1) * SUB, pair * LANES : (pair + 1) * LANES
            ]


def levels(devices):
    distances = [1 << bit for bit in range(1, devices.bit_length() - 1)]
    half = len(distances) // 2
    return distances[:half][::-1], distances[half:]


def find_tiles(devices, members, pairs, cols, mask, dest, own):
    slots = devices * CAP
    rank = cols % CAP
    source = (cols % slots) // CAP
    position = ((dest // members) * members + cols // slots) * CAP + rank
    return place_tiles(devices, pairs, source, position, mask, own)


def place_tiles(devices, pairs, source, position, mask, own):
    relative = source ^ own

    def collect(distances):
        return sum(((relative // distance) % 2) * (1 << order) for order, distance in enumerate(distances))

    near, far = levels(devices)
    count = 1 << len(near)
    even = source % 2 == 0
    piece = jnp.where(even, collect(far), collect(near))
    within = jnp.where(even, collect(near), collect(far))
    tile = (((relative % 2) * count + piece) * count + within) * pairs + position // 2
    swap = (position + lax.broadcasted_iota(jnp.int32, position.shape, 0)) % 2
    return jnp.where(mask != 0, tile * 2 + swap, 2 * devices * pairs)


def in_hbm(value):
    return pltpu.with_memory_space_constraint(value, pltpu.HBM)


def prepare(
    full, devices, members, perm_ref, rounded_ref, cols_hbm, mask_hbm, dest_hbm, smooth_hbm, right_hbm, blocks_hbm,
    own_ref, index_ref, x_ref, rp_ref, sbd_ref, blocks_ref,
    cols_ref, mask_ref, dest_ref, smooth_ref, right_ref, smooth_spread, right_spread, widened, sems,
):
    moves = [
        (cols_hbm, cols_ref), (mask_hbm, mask_ref), (dest_hbm, dest_ref),
        (right_hbm, right_ref), (smooth_hbm, smooth_ref), (blocks_hbm, blocks_ref),
    ]
    copies = [pltpu.make_async_copy(*move, sems.at[number]) for number, move in enumerate(moves)]
    for copy in copies:
        copy.start()
    rows, smooth_width = smooth_ref.shape
    block = LANES // 2
    half = smooth_width // LANES
    pairs = rows // 2
    lower = lax.broadcasted_iota(jnp.int32, (SUB, LANES), 1) < block
    low_half = lax.broadcasted_iota(jnp.int32, (half, LANES), 1) < block
    own_ref[...] = rounded_ref[...]
    for copy in copies[:3]:
        copy.wait()
    if full:
        index_ref[...] = find_tiles(
            devices, members, pairs, cols_ref[...], mask_ref[...], dest_ref[...],
            lax.axis_index("grp") * members + lax.axis_index("row"),
        )
    else:
        index_ref[...] = cols_ref[...]
    copies[3].wait()
    copied = right_copies(right_ref.shape[1])
    spread_rows(right_ref, right_spread, copied)
    copies[4].wait()
    spread_rows(smooth_ref, smooth_spread, smooth_copies(smooth_width))
    for pair in range(pairs):
        low, high = perm_ref[2 * pair], perm_ref[2 * pair + 1]
        rp_ref[pair] = jnp.where(
            lower,
            spread_row(right_spread, low, len(copied), 0, SUB),
            spread_row(right_spread, high, len(copied), SUB // 2, SUB),
        ).astype(jnp.bfloat16)
        base = pair * LANES
        for number, row in enumerate((low, high)):
            straight = spread_row(smooth_spread, row, half, 0, half)
            turned = pltpu.roll(straight, block, 1)
            first, second = (straight, turned) if number == 0 else (turned, straight)
            keep = low_half if number == 0 else jnp.logical_not(low_half)
            widened[pl.ds(base + number * block, half, stride=2), :] = jnp.where(keep, first, 0.0)
            widened[pl.ds(base + number * block + 1, half, stride=2), :] = jnp.where(keep, second, 0.0)
    for pair in range(pairs):
        sbd_ref[pair] = widened[pl.ds(pair * LANES, LANES), :].astype(jnp.bfloat16)
    for pair in range(pairs):
        x_ref[pair] = lax.dot_general(
            rp_ref[pair], sbd_ref[pair], TRANSPOSED, preferred_element_type=jnp.float32
        )
    copies[5].wait()


def later_sweep(piece_count, with_rounded, *refs):
    perm_ref, index_ref = refs[:2]
    pieces = refs[2 : 2 + piece_count]
    blocks, sbd_ref, rp_ref, x_ref = refs[2 + piece_count : 6 + piece_count]
    refs = refs[6 + piece_count :]
    out_ref = refs[0]
    rounded_ref = refs[1] if with_rounded else None
    tiles, defects = refs[2 if with_rounded else 1 :]
    pairs = x_ref.shape[0]
    _, block, width = blocks.shape
    bands = width // block

    start = 0
    for piece in pieces:
        size = piece.shape[0]
        tiles[pl.ds(start, size)] = piece[...]
        start += size
    tiles[start] = jnp.zeros((NRHS, LANES), jnp.bfloat16)

    lower = lax.broadcasted_iota(jnp.int32, (NRHS, LANES), 1) < block

    first_half = lax.broadcasted_iota(jnp.int32, (NRHS, LANES), 0) < NRHS // 2

    def fetch(row, band):
        entry = index_ref[band, row]
        tile = tiles[lax.shift_right_logical(entry, 1)].astype(jnp.float32)
        return pltpu.roll(tile, (entry & 1) * block, 1)

    def values(row):
        return [
            jnp.where(lower, fetch(row, 2 * half), fetch(row, 2 * half + 1)) for half in range(bands // 2)
        ]

    for pair in range(pairs):
        low, high = perm_ref[2 * pair], perm_ref[2 * pair + 1]
        gathered = jnp.concatenate(
            [
                jnp.concatenate(values(low), axis=1),
                jnp.concatenate(values(high), axis=1),
            ],
            axis=0,
        ).astype(jnp.bfloat16)
        weights = jnp.concatenate([blocks[low], blocks[high]], axis=0)
        applied = lax.dot_general(gathered, weights, TRANSPOSED, preferred_element_type=jnp.float32)
        image = jnp.where(lower, applied[:NRHS], applied[NRHS:])
        defects[pair] = (rp_ref[pair].astype(jnp.float32) - image).astype(jnp.bfloat16)

    for pair in range(pairs):
        x = x_ref[pair] + lax.dot_general(
            defects[pair], sbd_ref[pair], TRANSPOSED, preferred_element_type=jnp.float32
        )
        if with_rounded:
            out_ref[pair] = x
            rounded_ref[pair] = x.astype(jnp.bfloat16)
        else:
            crossed = pltpu.roll(pltpu.roll(x, block, 1), NRHS // 2, 0)
            out_ref[pair] = jnp.where(lower == first_half, x, crossed)


def lay_out(got_ref, out_ref):
    rows, width = out_ref.shape
    tiles = width // LANES
    for tile in range(tiles):
        out_ref[:, tile * LANES : (tile + 1) * LANES] = got_ref[pl.ds(tile, rows, stride=tiles), :]


def local(coarse_blocks, smoother, residual, dest, band_cols, band_mask):
    groups = lax.axis_size("grp")
    members = lax.axis_size("row")
    devices = groups * members
    rows, block, width = coarse_blocks.shape
    bands = band_cols.shape[1]
    pairs = rows // 2
    full = rows == devices * CAP
    smem = pl.BlockSpec(memory_space=pltpu.SMEM)
    vmem = pl.BlockSpec(memory_space=pltpu.VMEM)
    hbm = pl.BlockSpec(memory_space=pltpu.HBM)
    tile_shape = (pairs, NRHS, LANES)
    params = pltpu.CompilerParams(vmem_limit_bytes=VMEM_LIMIT)

    smooth_width, right_width = smoother.shape[1], residual.shape[1]
    smooth_rows = rows * len(smooth_copies(smooth_width))
    right_rows = rows * len(right_copies(right_width))
    perm, starts, rounded = pl.pallas_call(
        functools.partial(first_sweep, full),
        out_shape=(
            jax.ShapeDtypeStruct((rows,), jnp.int32),
            jax.ShapeDtypeStruct((devices,), jnp.int32),
            jax.ShapeDtypeStruct(tile_shape, jnp.bfloat16),
        ),
        in_specs=[hbm] * 3,
        out_specs=(smem, smem, vmem),
        scratch_shapes=[
            pltpu.SMEM((rows,), jnp.int32),
            pltpu.SMEM((devices,), jnp.int32),
            pltpu.VMEM(smoother.shape, jnp.bfloat16),
            pltpu.VMEM(residual.shape, jnp.bfloat16),
            pltpu.VMEM((smooth_rows, LANES), jnp.float32),
            pltpu.VMEM((right_rows, LANES), jnp.float32),
            pltpu.VMEM((pairs * SUB // 2, 2 * LANES), jnp.float32),
            pltpu.SemaphoreType.DMA((3,)),
        ],
        compiler_params=params,
        name="first_sweep",
    )(in_hbm(dest.reshape(rows)), in_hbm(smoother), in_hbm(residual))
    cols, mask = band_cols.T, band_mask.T
    if not full:
        slots = devices * CAP
        table = lax.all_gather(starts, ("grp", "row"), axis=0, tiled=True)
        source = (cols % slots) // CAP
        owner = (dest.T // members) * members + cols // slots
        position = jnp.take(table, source * devices + owner, mode="clip") + cols % CAP
        cols = place_tiles(devices, pairs, source, position, mask, lax.axis_index(("grp", "row")))
    own, index, x, right, smooth, blocks = pl.pallas_call(
        functools.partial(prepare, full, devices, members),
        out_shape=(
            jax.ShapeDtypeStruct(tile_shape, jnp.bfloat16),
            jax.ShapeDtypeStruct((bands, rows), jnp.int32),
            jax.ShapeDtypeStruct(tile_shape, jnp.float32),
            jax.ShapeDtypeStruct(tile_shape, jnp.bfloat16),
            jax.ShapeDtypeStruct((pairs, 2 * block, 2 * block), jnp.bfloat16),
            jax.ShapeDtypeStruct(coarse_blocks.shape, jnp.bfloat16),
        ),
        in_specs=[smem, vmem] + [hbm] * 6,
        out_specs=(vmem,) * 6,
        scratch_shapes=[
            pltpu.VMEM((bands, rows), jnp.int32),
            pltpu.VMEM((bands, rows), jnp.int32),
            pltpu.VMEM((1, rows), jnp.int32),
            pltpu.VMEM(smoother.shape, jnp.bfloat16),
            pltpu.VMEM(residual.shape, jnp.bfloat16),
            pltpu.VMEM((smooth_rows, LANES), jnp.float32),
            pltpu.VMEM((right_rows, LANES), jnp.float32),
            pltpu.VMEM((pairs * LANES, LANES), jnp.float32),
            pltpu.SemaphoreType.DMA((6,)),
        ],
        compiler_params=params,
        cost_estimate=pl.CostEstimate(flops=1 << 26, bytes_accessed=10 << 20, transcendentals=0),
        name="prepare",
    )(
        perm, rounded, in_hbm(cols), in_hbm(mask), in_hbm(dest.T),
        in_hbm(smoother), in_hbm(residual), in_hbm(coarse_blocks),
    )

    def exchange(value, distances):
        pairs_of = [(place, place ^ distances[place % 2]) for place in range(devices)]
        return lax.ppermute(value, ("grp", "row"), pairs_of)

    def direct(value, steps):
        held = [value]
        for place in range(1, 1 << len(steps)):
            even = sum(step[0] for order, step in enumerate(steps) if place >> order & 1)
            odd = sum(step[1] for order, step in enumerate(steps) if place >> order & 1)
            held.append(exchange(value, (even, odd)))
        return held

    def everywhere(value, own):
        even, odd = levels(devices)
        block = jnp.concatenate([own] + direct(value, list(zip(even, odd)))[1:], axis=0)
        near = direct(block, list(zip(odd, even)))
        return near + [exchange(part, (1, 1)) for part in near]

    def sweep(x, rounded, own, last):
        pieces = everywhere(rounded, own)
        outs = [jax.ShapeDtypeStruct(tile_shape, jnp.float32)]
        if not last:
            outs.append(jax.ShapeDtypeStruct(tile_shape, jnp.bfloat16))
        return pl.pallas_call(
            functools.partial(later_sweep, len(pieces), not last),
            out_shape=tuple(outs),
            in_specs=[smem, smem] + [vmem] * (len(pieces) + 4),
            out_specs=tuple([vmem] * len(outs)),
            scratch_shapes=[
                pltpu.VMEM((devices * pairs + 1, NRHS, LANES), jnp.bfloat16),
                pltpu.VMEM(tile_shape, jnp.bfloat16),
            ],
            compiler_params=params,
            name="later_sweep",
        )(perm, index, *pieces, blocks, smooth, right, x)

    x, rounded = sweep(x, rounded, own, False)
    (x,) = sweep(x, rounded, rounded, True)

    if not full:
        flat = x.reshape(rows, NRHS * block)
        following = jnp.concatenate([starts[1:], jnp.full((1,), rows, jnp.int32)])
        slots = devices * CAP
        wanted = starts[:, None] + jnp.arange(CAP, dtype=jnp.int32)[None, :]
        live = wanted < following[:, None]
        flat = jnp.where(
            live.reshape(slots, 1), jnp.take(flat, wanted.reshape(slots), axis=0, mode="clip"), 0.0
        )
        x = flat.reshape(devices, NRHS, LANES)
    got = lax.all_to_all(x, ("grp", "row"), split_axis=0, concat_axis=0, tiled=True)
    return pl.pallas_call(
        lay_out,
        out_shape=jax.ShapeDtypeStruct((devices * CAP, NRHS * block), jnp.float32),
        in_specs=[vmem],
        out_specs=vmem,
        compiler_params=params,
        name="lay_out",
    )(got.reshape(devices * NRHS, LANES))


def solution(mesh):
    in_specs = (
        P(("grp", "row"), None, None),
        P(("grp", "row"), None),
        P(("grp", "row"), None),
        P(("grp", "row"), None),
        P(("grp", "row"), None),
        P(("grp", "row"), None),
    )
    out_specs = P(("grp", "row"), None)
    return jax.shard_map(local, mesh=mesh, in_specs=in_specs, out_specs=out_specs, check_vma=False)
```

```python
import functools

import jax
import jax.numpy as jnp
from jax import lax
from jax.experimental import pallas as pl
from jax.experimental.pallas import tpu as pltpu
from jax.sharding import PartitionSpec as P

NRHS = 8
CAP = 2
LANES = 128
VMEM_LIMIT = 32 * 1024 * 1024

TRANSPOSED = (((1,), (1,)), ((), ()))
PLAIN = (((1,), (0,)), ((), ()))
SUB = 8


def spread_rows(source_ref, spread_ref, copies):
    rows, width = source_ref.shape
    tiles = width // LANES
    for top in range(rows // SUB):
        values = source_ref[top * SUB : (top + 1) * SUB, :].astype(jnp.float32)
        for place, (tile, turned) in enumerate(copies):
            piece = values[:, tile * LANES : (tile + 1) * LANES]
            if turned:
                piece = pltpu.roll(piece, LANES // 2, 1)
            spread_ref[pl.ds((top * len(copies) + place) * SUB, SUB), :] = piece


def spread_row(spread_ref, row, tiles, first, count):
    start = (row // SUB) * (tiles * SUB) + first * SUB + row % SUB
    return spread_ref[pl.ds(start, count, stride=SUB), :]


def smooth_copies(width):
    return [(tile, False) for tile in range(width // LANES)]


def right_copies(width):
    plain = [(tile, False) for tile in range(width // LANES)]
    turned = [(tile, True) for tile in range(width // LANES)]
    return plain + turned + plain


def sort_rows(full, dest_ref, perm_ref, starts_ref, count):
    rows = dest_ref.shape[0]
    owners = starts_ref.shape[0]
    if full:
        for owner in range(owners):
            count[owner] = owner * CAP
            starts_ref[owner] = owner * CAP
    else:

        def clear(owner, carry):
            count[owner] = 0
            return carry

        lax.fori_loop(0, owners, clear, 0)

        def tally(row, carry):
            count[dest_ref[row]] = count[dest_ref[row]] + 1
            return carry

        lax.fori_loop(0, rows, tally, 0)

        def start(owner, total):
            following = total + count[owner]
            starts_ref[owner] = total
            count[owner] = total
            return following

        lax.fori_loop(0, owners, start, jnp.int32(0))
    for row in range(rows):
        owner = dest_ref[row]
        position = count[owner]
        count[owner] = position + 1
        perm_ref[position] = row


def first_sweep(
    full, dest_hbm, smooth_hbm, right_hbm, perm_ref, starts_ref, xb_ref,
    dest_ref, count, smooth_ref, right_ref, smooth_spread, right_spread, collected, sems,
):
    copies = [
        pltpu.make_async_copy(dest_hbm, dest_ref, sems.at[0]),
        pltpu.make_async_copy(right_hbm, right_ref, sems.at[1]),
        pltpu.make_async_copy(smooth_hbm, smooth_ref, sems.at[2]),
    ]
    for copy in copies:
        copy.start()
    rows, smooth_width = smooth_ref.shape
    block = LANES // 2
    half = smooth_width // LANES
    quad = LANES // half
    lanes = lax.broadcasted_iota(jnp.int32, (2 * SUB, LANES), 1)
    lower = lanes[:SUB] < block
    width = quad * block
    held = lax.broadcasted_iota(jnp.int32, (width, width), 0)
    wanted = lax.broadcasted_iota(jnp.int32, (width, width), 1)
    placed = ((held % LANES) // half) * block + 2 * (held % half) + held // LANES
    order = jnp.where(placed == wanted, 1.0, 0.0).astype(jnp.bfloat16)

    copies[0].wait()
    sort_rows(full, dest_ref, perm_ref, starts_ref, count)
    copies[1].wait()
    copied = right_copies(right_ref.shape[1])
    spread_rows(right_ref, right_spread, copied)
    copies[2].wait()
    spread_rows(smooth_ref, smooth_spread, smooth_copies(smooth_width))

    for group in range(rows // quad):
        weights, values = [], []
        for member in range(quad):
            row = perm_ref[quad * group + member]
            weights.append(spread_row(smooth_spread, row, half, 0, half))
            straight = spread_row(right_spread, row, len(copied), 0, SUB)
            crossed = spread_row(right_spread, row, len(copied), SUB // 2, SUB)
            values += [jnp.where(lower, straight, 0.0), jnp.where(lower, 0.0, crossed)]
        products = lax.dot_general(
            jnp.concatenate(values, axis=0).astype(jnp.bfloat16),
            jnp.concatenate(weights, axis=0).astype(jnp.bfloat16),
            TRANSPOSED,
            preferred_element_type=jnp.float32,
        )
        own = products[: 2 * SUB]
        for member in range(1, quad):
            own = jnp.where(
                lanes // half == member, products[2 * SUB * member : 2 * SUB * (member + 1)], own
            )
        collected[pl.ds(group * SUB, SUB), :LANES] = own[:SUB]
        collected[pl.ds(group * SUB, SUB), LANES:] = own[SUB:]
    ordered = lax.dot_general(
        collected[...].astype(jnp.bfloat16), order, PLAIN, preferred_element_type=jnp.float32
    ).astype(jnp.bfloat16)
    for group in range(rows // quad):
        for pair in range(quad // 2):
            xb_ref[group * (quad // 2) + pair] = ordered[
                group * SUB : (group + 1) * SUB, pair * LANES : (pair + 1) * LANES
            ]


def levels(devices):
    distances = [1 << bit for bit in range(1, devices.bit_length() - 1)]
    half = len(distances) // 2
    return distances[:half][::-1], distances[half:]


def find_tiles(devices, members, pairs, cols, mask, dest, own):
    slots = devices * CAP
    rank = cols % CAP
    source = (cols % slots) // CAP
    position = ((dest // members) * members + cols // slots) * CAP + rank
    return place_tiles(devices, pairs, source, position, mask, own)


def place_tiles(devices, pairs, source, position, mask, own):
    relative = source ^ own

    def collect(distances):
        return sum(((relative // distance) % 2) * (1 << order) for order, distance in enumerate(distances))

    near, far = levels(devices)
    count = 1 << len(near)
    even = source % 2 == 0
    piece = count - 1 - jnp.where(even, collect(far), collect(near))
    within = jnp.where(even, collect(near), collect(far))
    within = jnp.where(within == 0, count - 1, jnp.where(within == count - 1, 0, within))
    tile = (((relative % 2) * count + piece) * count + within) * pairs + position // 2
    swap = (position + lax.broadcasted_iota(jnp.int32, position.shape, 0)) % 2
    return jnp.where(mask != 0, tile * 2 + swap, 2 * devices * pairs)


def in_hbm(value):
    return pltpu.with_memory_space_constraint(value, pltpu.HBM)


def locate(
    full, devices, members, rounded_ref, cols_hbm, mask_hbm, dest_hbm, own_ref, index_ref,
    cols_ref, mask_ref, dest_ref, lined, sems, line_sems,
):
    moves = [(cols_hbm, cols_ref), (mask_hbm, mask_ref), (dest_hbm, dest_ref)]
    copies = [pltpu.make_async_copy(*move, sems.at[number]) for number, move in enumerate(moves)]
    for copy in copies:
        copy.start()
    own_ref[...] = rounded_ref[...]
    for copy in copies:
        copy.wait()
    bands, rows = cols_ref.shape
    places = cols_ref[...]
    if full:
        places = find_tiles(
            devices, members, rows // 2, places, mask_ref[...], dest_ref[...],
            lax.axis_index("grp") * members + lax.axis_index("row"),
        )
    lined[:, :rows] = places
    lines = [
        pltpu.make_async_copy(lined.at[band], index_ref.at[pl.ds(band * LANES, LANES)], line_sems.at[band])
        for band in range(bands)
    ]
    for line in lines:
        line.start()
    for line in lines:
        line.wait()


def prepare(
    perm_ref, gathered_ref, smooth_hbm, right_hbm, blocks_hbm, own_ref, x_ref, rp_ref, sbd_ref, blocks_ref,
    smooth_ref, right_ref, smooth_spread, right_spread, widened, sems,
):
    moves = [(right_hbm, right_ref), (smooth_hbm, smooth_ref), (blocks_hbm, blocks_ref)]
    copies = [pltpu.make_async_copy(*move, sems.at[number]) for number, move in enumerate(moves)]
    for copy in copies:
        copy.start()
    own_ref[...] = gathered_ref[...]
    rows, smooth_width = smooth_ref.shape
    block = LANES // 2
    half = smooth_width // LANES
    pairs = rows // 2
    lower = lax.broadcasted_iota(jnp.int32, (SUB, LANES), 1) < block
    low_half = lax.broadcasted_iota(jnp.int32, (half, LANES), 1) < block
    copies[0].wait()
    copied = right_copies(right_ref.shape[1])
    spread_rows(right_ref, right_spread, copied)
    copies[1].wait()
    spread_rows(smooth_ref, smooth_spread, smooth_copies(smooth_width))
    for pair in range(pairs):
        low, high = perm_ref[2 * pair], perm_ref[2 * pair + 1]
        rp_ref[pair] = jnp.where(
            lower,
            spread_row(right_spread, low, len(copied), 0, SUB),
            spread_row(right_spread, high, len(copied), SUB // 2, SUB),
        ).astype(jnp.bfloat16)
        base = pair * LANES
        for number, row in enumerate((low, high)):
            straight = spread_row(smooth_spread, row, half, 0, half)
            turned = pltpu.roll(straight, block, 1)
            first, second = (straight, turned) if number == 0 else (turned, straight)
            keep = low_half if number == 0 else jnp.logical_not(low_half)
            widened[pl.ds(base + number * block, half, stride=2), :] = jnp.where(keep, first, 0.0)
            widened[pl.ds(base + number * block + 1, half, stride=2), :] = jnp.where(keep, second, 0.0)
    for pair in range(pairs):
        sbd_ref[pair] = widened[pl.ds(pair * LANES, LANES), :].T.astype(jnp.bfloat16)
    for pair in range(pairs):
        x_ref[pair] = lax.dot_general(
            rp_ref[pair], sbd_ref[pair], PLAIN, preferred_element_type=jnp.float32
        )
    copies[2].wait()


def later_sweep(piece_count, with_rounded, *refs):
    perm_ref, index_ref = refs[:2]
    pieces = refs[2 : 2 + piece_count]
    blocks, sbd_ref, rp_ref, x_ref = refs[2 + piece_count : 6 + piece_count]
    refs = refs[6 + piece_count :]
    out_ref = refs[0]
    rounded_ref = refs[1] if with_rounded else None
    tiles, defects = refs[2 if with_rounded else 1 :]
    pairs = x_ref.shape[0]
    rows, block, width = blocks.shape
    bands = width // block

    start = 0
    for piece in pieces:
        size = piece.shape[0]
        tiles[pl.ds(start, size)] = piece[...]
        start += size
    tiles[start] = jnp.zeros((NRHS, LANES), jnp.bfloat16)

    lower = lax.broadcasted_iota(jnp.int32, (NRHS, LANES), 1) < block

    first_half = lax.broadcasted_iota(jnp.int32, (NRHS, LANES), 0) < NRHS // 2

    def fetch(row, band):
        entry = index_ref[band * LANES + row]
        tile = tiles[lax.shift_right_logical(entry, 1)].astype(jnp.float32)
        return pltpu.roll(tile, (entry & 1) * block, 1)

    def values(row):
        return [
            jnp.where(lower, fetch(row, 2 * half), fetch(row, 2 * half + 1)) for half in range(bands // 2)
        ]

    for quad in range(rows // 4):
        members = [perm_ref[4 * quad + member] for member in range(4)]
        gathered = jnp.concatenate([jnp.concatenate(values(row), axis=1) for row in members], axis=0)
        weights = jnp.concatenate([blocks[row] for row in members], axis=0)
        applied = lax.dot_general(
            gathered.astype(jnp.bfloat16), weights, TRANSPOSED, preferred_element_type=jnp.float32
        )
        for half in range(2):
            pair = 2 * quad + half
            own = applied[2 * NRHS * half : 2 * NRHS * (half + 1), LANES * half : LANES * (half + 1)]
            image = jnp.where(lower, own[:NRHS], own[NRHS:])
            defects[pair] = (rp_ref[pair].astype(jnp.float32) - image).astype(jnp.bfloat16)

    for pair in range(pairs):
        x = x_ref[pair] + lax.dot_general(
            defects[pair], sbd_ref[pair], PLAIN, preferred_element_type=jnp.float32
        )
        if with_rounded:
            out_ref[pair] = x
            rounded_ref[pair] = x.astype(jnp.bfloat16)
        else:
            crossed = pltpu.roll(pltpu.roll(x, block, 1), NRHS // 2, 0)
            out_ref[pair] = jnp.where(lower == first_half, x, crossed)


def lay_out(got_ref, out_ref):
    rows, width = out_ref.shape
    tiles = width // LANES
    for tile in range(tiles):
        out_ref[:, tile * LANES : (tile + 1) * LANES] = got_ref[pl.ds(tile, rows, stride=tiles), :]


def local(coarse_blocks, smoother, residual, dest, band_cols, band_mask):
    groups = lax.axis_size("grp")
    members = lax.axis_size("row")
    devices = groups * members
    rows, block, width = coarse_blocks.shape
    bands = band_cols.shape[1]
    pairs = rows // 2
    full = rows == devices * CAP
    smem = pl.BlockSpec(memory_space=pltpu.SMEM)
    vmem = pl.BlockSpec(memory_space=pltpu.VMEM)
    hbm = pl.BlockSpec(memory_space=pltpu.HBM)
    tile_shape = (pairs, NRHS, LANES)
    params = pltpu.CompilerParams(vmem_limit_bytes=VMEM_LIMIT)

    smooth_width, right_width = smoother.shape[1], residual.shape[1]
    smooth_rows = rows * len(smooth_copies(smooth_width))
    right_rows = rows * len(right_copies(right_width))
    perm, starts, rounded = pl.pallas_call(
        functools.partial(first_sweep, full),
        out_shape=(
            jax.ShapeDtypeStruct((rows,), jnp.int32),
            jax.ShapeDtypeStruct((devices,), jnp.int32),
            jax.ShapeDtypeStruct(tile_shape, jnp.bfloat16),
        ),
        in_specs=[hbm] * 3,
        out_specs=(smem, smem, vmem),
        scratch_shapes=[
            pltpu.SMEM((rows,), jnp.int32),
            pltpu.SMEM((devices,), jnp.int32),
            pltpu.VMEM(smoother.shape, jnp.bfloat16),
            pltpu.VMEM(residual.shape, jnp.bfloat16),
            pltpu.VMEM((smooth_rows, LANES), jnp.float32),
            pltpu.VMEM((right_rows, LANES), jnp.float32),
            pltpu.VMEM((pairs * SUB // 2, 2 * LANES), jnp.float32),
            pltpu.SemaphoreType.DMA((3,)),
        ],
        compiler_params=params,
        name="first_sweep",
    )(in_hbm(dest.reshape(rows)), in_hbm(smoother), in_hbm(residual))
    cols, mask = band_cols.T, band_mask.T
    if not full:
        slots = devices * CAP
        table = lax.all_gather(starts, ("grp", "row"), axis=0, tiled=True)
        source = (cols % slots) // CAP
        owner = (dest.T // members) * members + cols // slots
        position = jnp.take(table, source * devices + owner, mode="clip") + cols % CAP
        cols = place_tiles(devices, pairs, source, position, mask, lax.axis_index(("grp", "row")))
    own, index = pl.pallas_call(
        functools.partial(locate, full, devices, members),
        out_shape=(
            jax.ShapeDtypeStruct(tile_shape, jnp.bfloat16),
            jax.ShapeDtypeStruct((bands * LANES,), jnp.int32),
        ),
        in_specs=[vmem] + [hbm] * 3,
        out_specs=(vmem, smem),
        scratch_shapes=[
            pltpu.VMEM((bands, rows), jnp.int32),
            pltpu.VMEM((bands, rows), jnp.int32),
            pltpu.VMEM((1, rows), jnp.int32),
            pltpu.VMEM((bands, LANES), jnp.int32),
            pltpu.SemaphoreType.DMA((3,)),
            pltpu.SemaphoreType.DMA((bands,)),
        ],
        compiler_params=params,
        cost_estimate=pl.CostEstimate(flops=1 << 20, bytes_accessed=2 << 20, transcendentals=0),
        name="locate",
    )(rounded, in_hbm(cols), in_hbm(mask), in_hbm(dest.T))

    def exchange(value, distances):
        pairs_of = [(place, place ^ distances[place % 2]) for place in range(devices)]
        return lax.ppermute(value, ("grp", "row"), pairs_of)

    def direct(value, steps):
        held = [value]
        for place in range(1, 1 << len(steps)):
            even = sum(step[0] for order, step in enumerate(steps) if place >> order & 1)
            odd = sum(step[1] for order, step in enumerate(steps) if place >> order & 1)
            held.append(exchange(value, (even, odd)))
        return held

    even, odd = levels(devices)

    def first_level(value, own):
        held = direct(value, list(zip(even, odd)))
        return jnp.concatenate([held[-1]] + held[1:-1] + [own], axis=0)

    def second_level(value, own):
        near = direct(value, list(zip(odd, even)))
        near, away = near[::-1], ([own] + near[1:])[::-1]
        return near + [exchange(part, (1, 1)) for part in away]

    gathered = first_level(rounded, own)
    own, x, right, smooth, blocks = pl.pallas_call(
        prepare,
        out_shape=(
            jax.ShapeDtypeStruct(gathered.shape, jnp.bfloat16),
            jax.ShapeDtypeStruct(tile_shape, jnp.float32),
            jax.ShapeDtypeStruct(tile_shape, jnp.bfloat16),
            jax.ShapeDtypeStruct((pairs, 2 * block, 2 * block), jnp.bfloat16),
            jax.ShapeDtypeStruct(coarse_blocks.shape, jnp.bfloat16),
        ),
        in_specs=[smem, vmem] + [hbm] * 3,
        out_specs=(vmem,) * 5,
        scratch_shapes=[
            pltpu.VMEM(smoother.shape, jnp.bfloat16),
            pltpu.VMEM(residual.shape, jnp.bfloat16),
            pltpu.VMEM((smooth_rows, LANES), jnp.float32),
            pltpu.VMEM((right_rows, LANES), jnp.float32),
            pltpu.VMEM((pairs * LANES, LANES), jnp.float32),
            pltpu.SemaphoreType.DMA((3,)),
        ],
        compiler_params=params,
        cost_estimate=pl.CostEstimate(flops=1 << 26, bytes_accessed=10 << 20, transcendentals=0),
        name="prepare",
    )(perm, gathered, in_hbm(smoother), in_hbm(residual), in_hbm(coarse_blocks))

    def sweep(x, value, own, last):
        pieces = second_level(value, own)
        outs = [jax.ShapeDtypeStruct(tile_shape, jnp.float32)]
        if not last:
            outs.append(jax.ShapeDtypeStruct(tile_shape, jnp.bfloat16))
        return pl.pallas_call(
            functools.partial(later_sweep, len(pieces), not last),
            out_shape=tuple(outs),
            in_specs=[smem, smem] + [vmem] * (len(pieces) + 4),
            out_specs=tuple([vmem] * len(outs)),
            scratch_shapes=[
                pltpu.VMEM((devices * pairs + 1, NRHS, LANES), jnp.bfloat16),
                pltpu.VMEM(tile_shape, jnp.bfloat16),
            ],
            compiler_params=params,
            name="later_sweep",
        )(perm, index, *pieces, blocks, smooth, right, x)

    x, rounded = sweep(x, gathered, own, False)
    gathered = first_level(rounded, rounded)
    (x,) = sweep(x, gathered, gathered, True)

    if not full:
        flat = x.reshape(rows, NRHS * block)
        following = jnp.concatenate([starts[1:], jnp.full((1,), rows, jnp.int32)])
        slots = devices * CAP
        wanted = starts[:, None] + jnp.arange(CAP, dtype=jnp.int32)[None, :]
        live = wanted < following[:, None]
        flat = jnp.where(
            live.reshape(slots, 1), jnp.take(flat, wanted.reshape(slots), axis=0, mode="clip"), 0.0
        )
        x = flat.reshape(devices, NRHS, LANES)
    got = lax.all_to_all(x, ("grp", "row"), split_axis=0, concat_axis=0, tiled=True)
    return pl.pallas_call(
        lay_out,
        out_shape=jax.ShapeDtypeStruct((devices * CAP, NRHS * block), jnp.float32),
        in_specs=[vmem],
        out_specs=vmem,
        compiler_params=params,
        name="lay_out",
    )(got.reshape(devices * NRHS, LANES))


def solution(mesh):
    in_specs = (
        P(("grp", "row"), None, None),
        P(("grp", "row"), None),
        P(("grp", "row"), None),
        P(("grp", "row"), None),
        P(("grp", "row"), None),
        P(("grp", "row"), None),
    )
    out_specs = P(("grp", "row"), None)
    return jax.shard_map(local, mesh=mesh, in_specs=in_specs, out_specs=out_specs, check_vma=False)
```

```python
import functools

import jax
import jax.numpy as jnp
from jax import lax
from jax.experimental import pallas as pl
from jax.experimental.pallas import tpu as pltpu
from jax.sharding import PartitionSpec as P

NRHS = 8
CAP = 2
LANES = 128
VMEM_LIMIT = 32 * 1024 * 1024

TRANSPOSED = (((1,), (1,)), ((), ()))
PLAIN = (((1,), (0,)), ((), ()))
SUB = 8


def spread_rows(source_ref, spread_ref, copies):
    rows, width = source_ref.shape
    tiles = width // LANES
    for top in range(rows // SUB):
        values = source_ref[top * SUB : (top + 1) * SUB, :].astype(jnp.float32)
        for place, (tile, turned) in enumerate(copies):
            piece = values[:, tile * LANES : (tile + 1) * LANES]
            if turned:
                piece = pltpu.roll(piece, LANES // 2, 1)
            spread_ref[pl.ds((top * len(copies) + place) * SUB, SUB), :] = piece


def spread_row(spread_ref, row, tiles, first, count):
    start = (row // SUB) * (tiles * SUB) + first * SUB + row % SUB
    return spread_ref[pl.ds(start, count, stride=SUB), :]


def smooth_copies(width):
    return [(tile, False) for tile in range(width // LANES)]


def right_copies(width):
    plain = [(tile, False) for tile in range(width // LANES)]
    turned = [(tile, True) for tile in range(width // LANES)]
    return plain + turned + plain


def sort_rows(full, dest_ref, perm_ref, starts_ref, count):
    rows = dest_ref.shape[0]
    owners = starts_ref.shape[0]
    if full:
        for owner in range(owners):
            count[owner] = owner * CAP
            starts_ref[owner] = owner * CAP
    else:

        def clear(owner, carry):
            count[owner] = 0
            return carry

        lax.fori_loop(0, owners, clear, 0)

        def tally(row, carry):
            count[dest_ref[row]] = count[dest_ref[row]] + 1
            return carry

        lax.fori_loop(0, rows, tally, 0)

        def start(owner, total):
            following = total + count[owner]
            starts_ref[owner] = total
            count[owner] = total
            return following

        lax.fori_loop(0, owners, start, jnp.int32(0))
    for row in range(rows):
        owner = dest_ref[row]
        position = count[owner]
        count[owner] = position + 1
        perm_ref[position] = row


def first_sweep(
    full, dest_hbm, smooth_hbm, right_hbm, perm_ref, starts_ref, xb_ref,
    dest_ref, count, smooth_ref, right_ref, smooth_spread, right_spread, collected, sems,
):
    copies = [
        pltpu.make_async_copy(dest_hbm, dest_ref, sems.at[0]),
        pltpu.make_async_copy(right_hbm, right_ref, sems.at[1]),
        pltpu.make_async_copy(smooth_hbm, smooth_ref, sems.at[2]),
    ]
    for copy in copies:
        copy.start()
    rows, smooth_width = smooth_ref.shape
    block = LANES // 2
    half = smooth_width // LANES
    quad = LANES // half
    lanes = lax.broadcasted_iota(jnp.int32, (2 * SUB, LANES), 1)
    lower = lanes[:SUB] < block
    width = quad * block
    held = lax.broadcasted_iota(jnp.int32, (width, width), 0)
    wanted = lax.broadcasted_iota(jnp.int32, (width, width), 1)
    placed = ((held % LANES) // half) * block + 2 * (held % half) + held // LANES
    order = jnp.where(placed == wanted, 1.0, 0.0).astype(jnp.bfloat16)

    copies[0].wait()
    sort_rows(full, dest_ref, perm_ref, starts_ref, count)
    copies[1].wait()
    copied = right_copies(right_ref.shape[1])
    spread_rows(right_ref, right_spread, copied)
    copies[2].wait()
    spread_rows(smooth_ref, smooth_spread, smooth_copies(smooth_width))

    for group in range(rows // quad):
        weights, values = [], []
        for member in range(quad):
            row = perm_ref[quad * group + member]
            weights.append(spread_row(smooth_spread, row, half, 0, half))
            straight = spread_row(right_spread, row, len(copied), 0, SUB)
            crossed = spread_row(right_spread, row, len(copied), SUB // 2, SUB)
            values += [jnp.where(lower, straight, 0.0), jnp.where(lower, 0.0, crossed)]
        products = lax.dot_general(
            jnp.concatenate(values, axis=0).astype(jnp.bfloat16),
            jnp.concatenate(weights, axis=0).astype(jnp.bfloat16),
            TRANSPOSED,
            preferred_element_type=jnp.float32,
        )
        own = products[: 2 * SUB]
        for member in range(1, quad):
            own = jnp.where(
                lanes // half == member, products[2 * SUB * member : 2 * SUB * (member + 1)], own
            )
        collected[pl.ds(group * SUB, SUB), :LANES] = own[:SUB]
        collected[pl.ds(group * SUB, SUB), LANES:] = own[SUB:]
    ordered = lax.dot_general(
        collected[...].astype(jnp.bfloat16), order, PLAIN, preferred_element_type=jnp.float32
    ).astype(jnp.bfloat16)
    for group in range(rows // quad):
        for pair in range(quad // 2):
            xb_ref[group * (quad // 2) + pair] = ordered[
                group * SUB : (group + 1) * SUB, pair * LANES : (pair + 1) * LANES
            ]


def levels(devices):
    distances = [1 << bit for bit in range(1, devices.bit_length() - 1)]
    half = len(distances) // 2
    return distances[:half][::-1], distances[half:]


def find_tiles(devices, members, pairs, cols, mask, dest, own):
    slots = devices * CAP
    rank = cols % CAP
    source = (cols % slots) // CAP
    position = ((dest // members) * members + cols // slots) * CAP + rank
    return place_tiles(devices, pairs, source, position, mask, own)


def place_tiles(devices, pairs, source, position, mask, own):
    relative = source ^ own

    def collect(distances):
        return sum(((relative // distance) % 2) * (1 << order) for order, distance in enumerate(distances))

    near, far = levels(devices)
    count = 1 << len(near)
    even = source % 2 == 0
    piece = count - 1 - jnp.where(even, collect(far), collect(near))
    within = jnp.where(even, collect(near), collect(far[::-1]))
    within = jnp.where(within == 0, count - 1, jnp.where(within == count - 1, 0, within))
    tile = (((relative % 2) * count + piece) * count + within) * pairs + position // 2
    swap = (position + lax.broadcasted_iota(jnp.int32, position.shape, 0)) % 2
    return jnp.where(mask != 0, tile * 2 + swap, 2 * devices * pairs)


def in_hbm(value):
    return pltpu.with_memory_space_constraint(value, pltpu.HBM)


def locate(
    full, devices, members, rounded_ref, cols_hbm, mask_hbm, dest_hbm, own_ref, index_ref,
    cols_ref, mask_ref, dest_ref, lined, sems, line_sems,
):
    moves = [(cols_hbm, cols_ref), (mask_hbm, mask_ref), (dest_hbm, dest_ref)]
    copies = [pltpu.make_async_copy(*move, sems.at[number]) for number, move in enumerate(moves)]
    for copy in copies:
        copy.start()
    own_ref[...] = rounded_ref[...]
    for copy in copies:
        copy.wait()
    bands, rows = cols_ref.shape
    places = cols_ref[...]
    if full:
        places = find_tiles(
            devices, members, rows // 2, places, mask_ref[...], dest_ref[...],
            lax.axis_index("grp") * members + lax.axis_index("row"),
        )
    lined[:, :rows] = places
    lines = [
        pltpu.make_async_copy(lined.at[band], index_ref.at[pl.ds(band * LANES, LANES)], line_sems.at[band])
        for band in range(bands)
    ]
    for line in lines:
        line.start()
    for line in lines:
        line.wait()


def duplicate(value_ref, out_ref):
    out_ref[...] = value_ref[...]


def prepare(
    perm_ref, gathered_ref, smooth_hbm, right_hbm, blocks_hbm, own_ref, x_ref, rp_ref, sbd_ref, blocks_ref,
    smooth_ref, right_ref, smooth_spread, right_spread, widened, sems,
):
    moves = [(right_hbm, right_ref), (smooth_hbm, smooth_ref), (blocks_hbm, blocks_ref)]
    copies = [pltpu.make_async_copy(*move, sems.at[number]) for number, move in enumerate(moves)]
    for copy in copies:
        copy.start()
    own_ref[...] = gathered_ref[...]
    rows, smooth_width = smooth_ref.shape
    block = LANES // 2
    half = smooth_width // LANES
    pairs = rows // 2
    lower = lax.broadcasted_iota(jnp.int32, (SUB, LANES), 1) < block
    low_half = lax.broadcasted_iota(jnp.int32, (half, LANES), 1) < block
    copies[0].wait()
    copied = right_copies(right_ref.shape[1])
    spread_rows(right_ref, right_spread, copied)
    copies[1].wait()
    spread_rows(smooth_ref, smooth_spread, smooth_copies(smooth_width))
    for pair in range(pairs):
        low, high = perm_ref[2 * pair], perm_ref[2 * pair + 1]
        rp_ref[pair] = jnp.where(
            lower,
            spread_row(right_spread, low, len(copied), 0, SUB),
            spread_row(right_spread, high, len(copied), SUB // 2, SUB),
        ).astype(jnp.bfloat16)
        base = pair * LANES
        for number, row in enumerate((low, high)):
            straight = spread_row(smooth_spread, row, half, 0, half)
            turned = pltpu.roll(straight, block, 1)
            first, second = (straight, turned) if number == 0 else (turned, straight)
            keep = low_half if number == 0 else jnp.logical_not(low_half)
            widened[pl.ds(base + number * block, half, stride=2), :] = jnp.where(keep, first, 0.0)
            widened[pl.ds(base + number * block + 1, half, stride=2), :] = jnp.where(keep, second, 0.0)
    for pair in range(pairs):
        sbd_ref[pair] = widened[pl.ds(pair * LANES, LANES), :].T.astype(jnp.bfloat16)
    for pair in range(pairs):
        x_ref[pair] = lax.dot_general(
            rp_ref[pair], sbd_ref[pair], PLAIN, preferred_element_type=jnp.float32
        )
    copies[2].wait()


def later_sweep(plan, piece_count, with_rounded, *refs):
    perm_ref, index_ref = refs[:2]
    pieces = refs[2 : 2 + piece_count]
    blocks, sbd_ref, rp_ref, x_ref = refs[2 + piece_count : 6 + piece_count]
    refs = refs[6 + piece_count :]
    out_ref = refs[0]
    rounded_ref = refs[1] if with_rounded else None
    tiles, defects = refs[2 if with_rounded else 1 :]
    pairs = x_ref.shape[0]
    rows, block, width = blocks.shape
    bands = width // block

    for number, start, size, place in plan:
        tiles[pl.ds(place * pairs, size * pairs)] = pieces[number][pl.ds(start * pairs, size * pairs)]
    tiles[tiles.shape[0] - 1] = jnp.zeros((NRHS, LANES), jnp.bfloat16)

    lower = lax.broadcasted_iota(jnp.int32, (NRHS, LANES), 1) < block

    first_half = lax.broadcasted_iota(jnp.int32, (NRHS, LANES), 0) < NRHS // 2

    def fetch(row, band):
        entry = index_ref[band * LANES + row]
        tile = tiles[lax.shift_right_logical(entry, 1)].astype(jnp.float32)
        return pltpu.roll(tile, (entry & 1) * block, 1)

    def values(row):
        return [
            jnp.where(lower, fetch(row, 2 * half), fetch(row, 2 * half + 1)) for half in range(bands // 2)
        ]

    for quad in range(rows // 4):
        members = [perm_ref[4 * quad + member] for member in range(4)]
        gathered = jnp.concatenate([jnp.concatenate(values(row), axis=1) for row in members], axis=0)
        weights = jnp.concatenate([blocks[row] for row in members], axis=0)
        applied = lax.dot_general(
            gathered.astype(jnp.bfloat16), weights, TRANSPOSED, preferred_element_type=jnp.float32
        )
        for half in range(2):
            pair = 2 * quad + half
            own = applied[2 * NRHS * half : 2 * NRHS * (half + 1), LANES * half : LANES * (half + 1)]
            image = jnp.where(lower, own[:NRHS], own[NRHS:])
            defects[pair] = (rp_ref[pair].astype(jnp.float32) - image).astype(jnp.bfloat16)

    for pair in range(pairs):
        x = x_ref[pair] + lax.dot_general(
            defects[pair], sbd_ref[pair], PLAIN, preferred_element_type=jnp.float32
        )
        if with_rounded:
            out_ref[pair] = x
            rounded_ref[pair] = x.astype(jnp.bfloat16)
        else:
            crossed = pltpu.roll(pltpu.roll(x, block, 1), NRHS // 2, 0)
            out_ref[pair] = jnp.where(lower == first_half, x, crossed)


def lay_out(got_ref, out_ref):
    rows, width = out_ref.shape
    tiles = width // LANES
    for tile in range(tiles):
        out_ref[:, tile * LANES : (tile + 1) * LANES] = got_ref[pl.ds(tile, rows, stride=tiles), :]


def local(coarse_blocks, smoother, residual, dest, band_cols, band_mask):
    groups = lax.axis_size("grp")
    members = lax.axis_size("row")
    devices = groups * members
    rows, block, width = coarse_blocks.shape
    bands = band_cols.shape[1]
    pairs = rows // 2
    full = rows == devices * CAP
    smem = pl.BlockSpec(memory_space=pltpu.SMEM)
    vmem = pl.BlockSpec(memory_space=pltpu.VMEM)
    hbm = pl.BlockSpec(memory_space=pltpu.HBM)
    tile_shape = (pairs, NRHS, LANES)
    params = pltpu.CompilerParams(vmem_limit_bytes=VMEM_LIMIT)

    smooth_width, right_width = smoother.shape[1], residual.shape[1]
    smooth_rows = rows * len(smooth_copies(smooth_width))
    right_rows = rows * len(right_copies(right_width))
    perm, starts, rounded = pl.pallas_call(
        functools.partial(first_sweep, full),
        out_shape=(
            jax.ShapeDtypeStruct((rows,), jnp.int32),
            jax.ShapeDtypeStruct((devices,), jnp.int32),
            jax.ShapeDtypeStruct(tile_shape, jnp.bfloat16),
        ),
        in_specs=[hbm] * 3,
        out_specs=(smem, smem, vmem),
        scratch_shapes=[
            pltpu.SMEM((rows,), jnp.int32),
            pltpu.SMEM((devices,), jnp.int32),
            pltpu.VMEM(smoother.shape, jnp.bfloat16),
            pltpu.VMEM(residual.shape, jnp.bfloat16),
            pltpu.VMEM((smooth_rows, LANES), jnp.float32),
            pltpu.VMEM((right_rows, LANES), jnp.float32),
            pltpu.VMEM((pairs * SUB // 2, 2 * LANES), jnp.float32),
            pltpu.SemaphoreType.DMA((3,)),
        ],
        compiler_params=params,
        name="first_sweep",
    )(in_hbm(dest.reshape(rows)), in_hbm(smoother), in_hbm(residual))
    cols, mask = band_cols.T, band_mask.T
    if not full:
        slots = devices * CAP
        table = lax.all_gather(starts, ("grp", "row"), axis=0, tiled=True)
        source = (cols % slots) // CAP
        owner = (dest.T // members) * members + cols // slots
        position = jnp.take(table, source * devices + owner, mode="clip") + cols % CAP
        cols = place_tiles(devices, pairs, source, position, mask, lax.axis_index(("grp", "row")))
    own, index = pl.pallas_call(
        functools.partial(locate, full, devices, members),
        out_shape=(
            jax.ShapeDtypeStruct(tile_shape, jnp.bfloat16),
            jax.ShapeDtypeStruct((bands * LANES,), jnp.int32),
        ),
        in_specs=[vmem] + [hbm] * 3,
        out_specs=(vmem, smem),
        scratch_shapes=[
            pltpu.VMEM((bands, rows), jnp.int32),
            pltpu.VMEM((bands, rows), jnp.int32),
            pltpu.VMEM((1, rows), jnp.int32),
            pltpu.VMEM((bands, LANES), jnp.int32),
            pltpu.SemaphoreType.DMA((3,)),
            pltpu.SemaphoreType.DMA((bands,)),
        ],
        compiler_params=params,
        cost_estimate=pl.CostEstimate(flops=1 << 20, bytes_accessed=2 << 20, transcendentals=0),
        name="locate",
    )(rounded, in_hbm(cols), in_hbm(mask), in_hbm(dest.T))

    def exchange(value, distances):
        pairs_of = [(place, place ^ distances[place % 2]) for place in range(devices)]
        return lax.ppermute(value, ("grp", "row"), pairs_of)

    def direct(value, steps):
        held = [value]
        for place in range(1, 1 << len(steps)):
            even = sum(step[0] for order, step in enumerate(steps) if place >> order & 1)
            odd = sum(step[1] for order, step in enumerate(steps) if place >> order & 1)
            held.append(exchange(value, (even, odd)))
        return held

    even, odd = levels(devices)
    count = 1 << len(even)

    def first_level(value, own):
        held = direct(value, list(zip(even, odd[::-1])))
        return jnp.concatenate([held[-1]] + held[1:-1] + [own], axis=0)

    def second_level(value, own):
        near = direct(value, list(zip(odd, even)))
        near, away = near[::-1], ([own] + near[1:])[::-1]
        plan = [(number, 0, count, number * count) for number in range(2 * count)]
        return plan, near + [exchange(part, (1, 1)) for part in away]

    def both_levels(value):
        ahead = direct(value, list(zip(even, odd[::-1])))
        copy = pl.pallas_call(
            duplicate,
            out_shape=jax.ShapeDtypeStruct(tile_shape, jnp.bfloat16),
            in_specs=[vmem],
            out_specs=vmem,
            compiler_params=params,
            name="duplicate",
        )(value)
        aside = direct(copy, list(zip(odd, even)))
        ahead = jnp.concatenate([ahead[-1]] + ahead[1:-1], axis=0)
        aside = jnp.concatenate([aside[-1]] + aside[1:-1] + [copy], axis=0)
        near = [aside, ahead] + direct(ahead, list(zip(odd, even)))[:0:-1]
        plan = []
        for core in range(2):
            base, number = core * count * count, core * len(near)
            for place in range(count):
                row = {0: 0, count - 1: count - 1}.get(place, count - 1 - place)
                plan.append((number, place, 1, base + row * count + count - 1))
            plan.append((number + 1, 0, count - 1, base + (count - 1) * count))
            for row in range(count - 1):
                plan.append((number + 2 + row, 0, count - 1, base + row * count))
        return plan, near + [exchange(part, (1, 1)) for part in near]

    gathered = first_level(rounded, own)
    own, x, right, smooth, blocks = pl.pallas_call(
        prepare,
        out_shape=(
            jax.ShapeDtypeStruct(gathered.shape, jnp.bfloat16),
            jax.ShapeDtypeStruct(tile_shape, jnp.float32),
            jax.ShapeDtypeStruct(tile_shape, jnp.bfloat16),
            jax.ShapeDtypeStruct((pairs, 2 * block, 2 * block), jnp.bfloat16),
            jax.ShapeDtypeStruct(coarse_blocks.shape, jnp.bfloat16),
        ),
        in_specs=[smem, vmem] + [hbm] * 3,
        out_specs=(vmem,) * 5,
        scratch_shapes=[
            pltpu.VMEM(smoother.shape, jnp.bfloat16),
            pltpu.VMEM(residual.shape, jnp.bfloat16),
            pltpu.VMEM((smooth_rows, LANES), jnp.float32),
            pltpu.VMEM((right_rows, LANES), jnp.float32),
            pltpu.VMEM((pairs * LANES, LANES), jnp.float32),
            pltpu.SemaphoreType.DMA((3,)),
        ],
        compiler_params=params,
        cost_estimate=pl.CostEstimate(flops=1 << 26, bytes_accessed=10 << 20, transcendentals=0),
        name="prepare",
    )(perm, gathered, in_hbm(smoother), in_hbm(residual), in_hbm(coarse_blocks))

    def sweep(x, plan, pieces, last):
        outs = [jax.ShapeDtypeStruct(tile_shape, jnp.float32)]
        if not last:
            outs.append(jax.ShapeDtypeStruct(tile_shape, jnp.bfloat16))
        return pl.pallas_call(
            functools.partial(later_sweep, plan, len(pieces), not last),
            out_shape=tuple(outs),
            in_specs=[smem, smem] + [vmem] * (len(pieces) + 4),
            out_specs=tuple([vmem] * len(outs)),
            scratch_shapes=[
                pltpu.VMEM((devices * pairs + 1, NRHS, LANES), jnp.bfloat16),
                pltpu.VMEM(tile_shape, jnp.bfloat16),
            ],
            compiler_params=params,
            name="later_sweep",
        )(perm, index, *pieces, blocks, smooth, right, x)

    x, rounded = sweep(x, *second_level(gathered, own), False)
    (x,) = sweep(x, *both_levels(rounded), True)

    if not full:
        flat = x.reshape(rows, NRHS * block)
        following = jnp.concatenate([starts[1:], jnp.full((1,), rows, jnp.int32)])
        slots = devices * CAP
        wanted = starts[:, None] + jnp.arange(CAP, dtype=jnp.int32)[None, :]
        live = wanted < following[:, None]
        flat = jnp.where(
            live.reshape(slots, 1), jnp.take(flat, wanted.reshape(slots), axis=0, mode="clip"), 0.0
        )
        x = flat.reshape(devices, NRHS, LANES)
    got = lax.all_to_all(x, ("grp", "row"), split_axis=0, concat_axis=0, tiled=True)
    return pl.pallas_call(
        lay_out,
        out_shape=jax.ShapeDtypeStruct((devices * CAP, NRHS * block), jnp.float32),
        in_specs=[vmem],
        out_specs=vmem,
        compiler_params=params,
        name="lay_out",
    )(got.reshape(devices * NRHS, LANES))


def solution(mesh):
    in_specs = (
        P(("grp", "row"), None, None),
        P(("grp", "row"), None),
        P(("grp", "row"), None),
        P(("grp", "row"), None),
        P(("grp", "row"), None),
        P(("grp", "row"), None),
    )
    out_specs = P(("grp", "row"), None)
    return jax.shard_map(local, mesh=mesh, in_specs=in_specs, out_specs=out_specs, check_vma=False)
```

```python
import functools

import jax
import jax.numpy as jnp
from jax import lax
from jax.experimental import pallas as pl
from jax.experimental.pallas import tpu as pltpu
from jax.sharding import PartitionSpec as P

NRHS = 8
CAP = 2
LANES = 128
VMEM_LIMIT = 32 * 1024 * 1024

TRANSPOSED = (((1,), (1,)), ((), ()))
PLAIN = (((1,), (0,)), ((), ()))
SUB = 8


def spread_rows(source_ref, spread_ref, copies):
    rows, width = source_ref.shape
    tiles = width // LANES
    for top in range(rows // SUB):
        values = source_ref[top * SUB : (top + 1) * SUB, :].astype(jnp.float32)
        for place, (tile, turned) in enumerate(copies):
            piece = values[:, tile * LANES : (tile + 1) * LANES]
            if turned:
                piece = pltpu.roll(piece, LANES // 2, 1)
            spread_ref[pl.ds((top * len(copies) + place) * SUB, SUB), :] = piece


def spread_row(spread_ref, row, tiles, first, count):
    start = (row // SUB) * (tiles * SUB) + first * SUB + row % SUB
    return spread_ref[pl.ds(start, count, stride=SUB), :]


def smooth_copies(width):
    return [(tile, False) for tile in range(width // LANES)]


def right_copies(width):
    plain = [(tile, False) for tile in range(width // LANES)]
    turned = [(tile, True) for tile in range(width // LANES)]
    return plain + turned + plain


def sort_rows(full, dest_ref, perm_ref, starts_ref, count):
    rows = dest_ref.shape[0]
    owners = starts_ref.shape[0]
    if full:
        for owner in range(owners):
            count[owner] = owner * CAP
            starts_ref[owner] = owner * CAP
    else:

        def clear(owner, carry):
            count[owner] = 0
            return carry

        lax.fori_loop(0, owners, clear, 0)

        def tally(row, carry):
            count[dest_ref[row]] = count[dest_ref[row]] + 1
            return carry

        lax.fori_loop(0, rows, tally, 0)

        def start(owner, total):
            following = total + count[owner]
            starts_ref[owner] = total
            count[owner] = total
            return following

        lax.fori_loop(0, owners, start, jnp.int32(0))
    for row in range(rows):
        owner = dest_ref[row]
        position = count[owner]
        count[owner] = position + 1
        perm_ref[position] = row


def first_sweep(
    full, dest_hbm, smooth_hbm, right_hbm, perm_ref, starts_ref, xb_ref,
    dest_ref, count, smooth_ref, right_ref, smooth_spread, right_spread, collected, sems,
):
    copies = [
        pltpu.make_async_copy(dest_hbm, dest_ref, sems.at[0]),
        pltpu.make_async_copy(right_hbm, right_ref, sems.at[1]),
        pltpu.make_async_copy(smooth_hbm, smooth_ref, sems.at[2]),
    ]
    for copy in copies:
        copy.start()
    rows, smooth_width = smooth_ref.shape
    block = LANES // 2
    half = smooth_width // LANES
    quad = LANES // half
    lanes = lax.broadcasted_iota(jnp.int32, (2 * SUB, LANES), 1)
    lower = lanes[:SUB] < block
    width = quad * block
    held = lax.broadcasted_iota(jnp.int32, (width, width), 0)
    wanted = lax.broadcasted_iota(jnp.int32, (width, width), 1)
    placed = ((held % LANES) // half) * block + 2 * (held % half) + held // LANES
    order = jnp.where(placed == wanted, 1.0, 0.0).astype(jnp.bfloat16)

    copies[0].wait()
    sort_rows(full, dest_ref, perm_ref, starts_ref, count)
    copies[1].wait()
    copied = right_copies(right_ref.shape[1])
    spread_rows(right_ref, right_spread, copied)
    copies[2].wait()
    spread_rows(smooth_ref, smooth_spread, smooth_copies(smooth_width))

    for group in range(rows // quad):
        weights, values = [], []
        for member in range(quad):
            row = perm_ref[quad * group + member]
            weights.append(spread_row(smooth_spread, row, half, 0, half))
            straight = spread_row(right_spread, row, len(copied), 0, SUB)
            crossed = spread_row(right_spread, row, len(copied), SUB // 2, SUB)
            values += [jnp.where(lower, straight, 0.0), jnp.where(lower, 0.0, crossed)]
        products = lax.dot_general(
            jnp.concatenate(values, axis=0).astype(jnp.bfloat16),
            jnp.concatenate(weights, axis=0).astype(jnp.bfloat16),
            TRANSPOSED,
            preferred_element_type=jnp.float32,
        )
        own = products[: 2 * SUB]
        for member in range(1, quad):
            own = jnp.where(
                lanes // half == member, products[2 * SUB * member : 2 * SUB * (member + 1)], own
            )
        collected[pl.ds(group * SUB, SUB), :LANES] = own[:SUB]
        collected[pl.ds(group * SUB, SUB), LANES:] = own[SUB:]
    ordered = lax.dot_general(
        collected[...].astype(jnp.bfloat16), order, PLAIN, preferred_element_type=jnp.float32
    ).astype(jnp.bfloat16)
    for group in range(rows // quad):
        for pair in range(quad // 2):
            xb_ref[group * (quad // 2) + pair] = ordered[
                group * SUB : (group + 1) * SUB, pair * LANES : (pair + 1) * LANES
            ]


def levels(devices):
    distances = [1 << bit for bit in range(1, devices.bit_length() - 1)]
    half = len(distances) // 2
    return distances[:half][::-1], distances[half:]


def find_tiles(devices, members, pairs, cols, mask, dest, own):
    slots = devices * CAP
    rank = cols % CAP
    source = (cols % slots) // CAP
    position = ((dest // members) * members + cols // slots) * CAP + rank
    return place_tiles(devices, pairs, source, position, mask, own)


def place_tiles(devices, pairs, source, position, mask, own):
    relative = source ^ own

    def collect(distances):
        return sum(((relative // distance) % 2) * (1 << order) for order, distance in enumerate(distances))

    near, far = levels(devices)
    count = 1 << len(near)
    even = source % 2 == 0
    piece = count - 1 - jnp.where(even, collect(far), collect(near))
    within = jnp.where(even, collect(near), collect(far[::-1]))
    within = jnp.where(within == 0, count - 1, jnp.where(within == count - 1, 0, within))
    tile = (((relative % 2) * count + piece) * count + within) * pairs + position // 2
    swap = (position + lax.broadcasted_iota(jnp.int32, position.shape, 0)) % 2
    return jnp.where(mask != 0, tile * 2 + swap, 2 * devices * pairs)


def in_hbm(value):
    return pltpu.with_memory_space_constraint(value, pltpu.HBM)


def locate(
    full, devices, members, rounded_ref, cols_hbm, mask_hbm, dest_hbm, own_ref, index_ref,
    cols_ref, mask_ref, dest_ref, lined, sems, line_sems,
):
    moves = [(cols_hbm, cols_ref), (mask_hbm, mask_ref), (dest_hbm, dest_ref)]
    copies = [pltpu.make_async_copy(*move, sems.at[number]) for number, move in enumerate(moves)]
    for copy in copies:
        copy.start()
    own_ref[...] = rounded_ref[...]
    for copy in copies:
        copy.wait()
    bands, rows = cols_ref.shape
    places = cols_ref[...]
    if full:
        places = find_tiles(
            devices, members, rows // 2, places, mask_ref[...], dest_ref[...],
            lax.axis_index("grp") * members + lax.axis_index("row"),
        )
    lined[:, :rows] = places
    lines = [
        pltpu.make_async_copy(lined.at[band], index_ref.at[pl.ds(band * LANES, LANES)], line_sems.at[band])
        for band in range(bands)
    ]
    for line in lines:
        line.start()
    for line in lines:
        line.wait()


def duplicate(value_ref, out_ref):
    out_ref[...] = value_ref[...]


def prepare(
    perm_ref, gathered_ref, smooth_hbm, right_hbm, blocks_hbm, own_ref, x_ref, rp_ref, sbd_ref, blocks_ref,
    smooth_ref, right_ref, smooth_spread, right_spread, widened, sems,
):
    moves = [(right_hbm, right_ref), (smooth_hbm, smooth_ref), (blocks_hbm, blocks_ref)]
    copies = [pltpu.make_async_copy(*move, sems.at[number]) for number, move in enumerate(moves)]
    for copy in copies:
        copy.start()
    own_ref[...] = gathered_ref[...]
    rows, smooth_width = smooth_ref.shape
    block = LANES // 2
    half = smooth_width // LANES
    pairs = rows // 2
    lower = lax.broadcasted_iota(jnp.int32, (SUB, LANES), 1) < block
    low_half = lax.broadcasted_iota(jnp.int32, (half, LANES), 1) < block
    copies[0].wait()
    copied = right_copies(right_ref.shape[1])
    spread_rows(right_ref, right_spread, copied)
    copies[1].wait()
    spread_rows(smooth_ref, smooth_spread, smooth_copies(smooth_width))
    for pair in range(pairs):
        low, high = perm_ref[2 * pair], perm_ref[2 * pair + 1]
        rp_ref[pair] = jnp.where(
            lower,
            spread_row(right_spread, low, len(copied), 0, SUB),
            spread_row(right_spread, high, len(copied), SUB // 2, SUB),
        ).astype(jnp.bfloat16)
        base = pair * LANES
        for number, row in enumerate((low, high)):
            straight = spread_row(smooth_spread, row, half, 0, half)
            turned = pltpu.roll(straight, block, 1)
            first, second = (straight, turned) if number == 0 else (turned, straight)
            keep = low_half if number == 0 else jnp.logical_not(low_half)
            widened[pl.ds(base + number * block, half, stride=2), :] = jnp.where(keep, first, 0.0)
            widened[pl.ds(base + number * block + 1, half, stride=2), :] = jnp.where(keep, second, 0.0)
    for pair in range(pairs):
        sbd_ref[pair] = widened[pl.ds(pair * LANES, LANES), :].T.astype(jnp.bfloat16)
    for pair in range(pairs):
        x_ref[pair] = lax.dot_general(
            rp_ref[pair], sbd_ref[pair], PLAIN, preferred_element_type=jnp.float32
        )
    copies[2].wait()


def later_sweep(plan, piece_count, with_rounded, *refs):
    perm_ref, index_ref = refs[:2]
    pieces = refs[2 : 2 + piece_count]
    blocks, sbd_ref, rp_ref, x_ref = refs[2 + piece_count : 6 + piece_count]
    refs = refs[6 + piece_count :]
    out_ref = refs[0]
    rounded_ref = refs[1] if with_rounded else None
    tiles, defects = refs[2 if with_rounded else 1 :]
    pairs = x_ref.shape[0]
    rows, block, width = blocks.shape
    bands = width // block

    for number, start, size, place in plan:
        tiles[pl.ds(place * pairs, size * pairs)] = pieces[number][pl.ds(start * pairs, size * pairs)]
    tiles[tiles.shape[0] - 1] = jnp.zeros((NRHS, LANES), jnp.bfloat16)

    lower = lax.broadcasted_iota(jnp.int32, (NRHS, LANES), 1) < block

    first_half = lax.broadcasted_iota(jnp.int32, (NRHS, LANES), 0) < NRHS // 2

    def fetch(row, band):
        entry = index_ref[band * LANES + row]
        tile = tiles[lax.shift_right_logical(entry, 1)].astype(jnp.float32)
        return pltpu.roll(tile, (entry & 1) * block, 1)

    def values(row):
        return [
            jnp.where(lower, fetch(row, 2 * half), fetch(row, 2 * half + 1)) for half in range(bands // 2)
        ]

    for group in range(rows // 8):
        members = [perm_ref[8 * group + member] for member in range(8)]
        gathered = jnp.concatenate([jnp.concatenate(values(row), axis=1) for row in members], axis=0)
        weights = jnp.concatenate([blocks[row] for row in members], axis=0)
        applied = lax.dot_general(
            gathered.astype(jnp.bfloat16), weights, TRANSPOSED, preferred_element_type=jnp.float32
        )
        for half in range(4):
            pair = 4 * group + half
            own = applied[2 * NRHS * half : 2 * NRHS * (half + 1), LANES * half : LANES * (half + 1)]
            image = jnp.where(lower, own[:NRHS], own[NRHS:])
            defects[pair] = (rp_ref[pair].astype(jnp.float32) - image).astype(jnp.bfloat16)

    for pair in range(pairs):
        x = x_ref[pair] + lax.dot_general(
            defects[pair], sbd_ref[pair], PLAIN, preferred_element_type=jnp.float32
        )
        if with_rounded:
            out_ref[pair] = x
            rounded_ref[pair] = x.astype(jnp.bfloat16)
        else:
            crossed = pltpu.roll(pltpu.roll(x, block, 1), NRHS // 2, 0)
            out_ref[pair] = jnp.where(lower == first_half, x, crossed)


def lay_out(got_ref, out_ref):
    rows, width = out_ref.shape
    tiles = width // LANES
    for tile in range(tiles):
        out_ref[:, tile * LANES : (tile + 1) * LANES] = got_ref[pl.ds(tile, rows, stride=tiles), :]


def local(coarse_blocks, smoother, residual, dest, band_cols, band_mask):
    groups = lax.axis_size("grp")
    members = lax.axis_size("row")
    devices = groups * members
    rows, block, width = coarse_blocks.shape
    bands = band_cols.shape[1]
    pairs = rows // 2
    full = rows == devices * CAP
    smem = pl.BlockSpec(memory_space=pltpu.SMEM)
    vmem = pl.BlockSpec(memory_space=pltpu.VMEM)
    hbm = pl.BlockSpec(memory_space=pltpu.HBM)
    tile_shape = (pairs, NRHS, LANES)
    params = pltpu.CompilerParams(vmem_limit_bytes=VMEM_LIMIT)

    smooth_width, right_width = smoother.shape[1], residual.shape[1]
    smooth_rows = rows * len(smooth_copies(smooth_width))
    right_rows = rows * len(right_copies(right_width))
    perm, starts, rounded = pl.pallas_call(
        functools.partial(first_sweep, full),
        out_shape=(
            jax.ShapeDtypeStruct((rows,), jnp.int32),
            jax.ShapeDtypeStruct((devices,), jnp.int32),
            jax.ShapeDtypeStruct(tile_shape, jnp.bfloat16),
        ),
        in_specs=[hbm] * 3,
        out_specs=(smem, smem, vmem),
        scratch_shapes=[
            pltpu.SMEM((rows,), jnp.int32),
            pltpu.SMEM((devices,), jnp.int32),
            pltpu.VMEM(smoother.shape, jnp.bfloat16),
            pltpu.VMEM(residual.shape, jnp.bfloat16),
            pltpu.VMEM((smooth_rows, LANES), jnp.float32),
            pltpu.VMEM((right_rows, LANES), jnp.float32),
            pltpu.VMEM((pairs * SUB // 2, 2 * LANES), jnp.float32),
            pltpu.SemaphoreType.DMA((3,)),
        ],
        compiler_params=params,
        name="first_sweep",
    )(in_hbm(dest.reshape(rows)), in_hbm(smoother), in_hbm(residual))
    cols, mask = band_cols.T, band_mask.T
    if not full:
        slots = devices * CAP
        table = lax.all_gather(starts, ("grp", "row"), axis=0, tiled=True)
        source = (cols % slots) // CAP
        owner = (dest.T // members) * members + cols // slots
        position = jnp.take(table, source * devices + owner, mode="clip") + cols % CAP
        cols = place_tiles(devices, pairs, source, position, mask, lax.axis_index(("grp", "row")))
    own, index = pl.pallas_call(
        functools.partial(locate, full, devices, members),
        out_shape=(
            jax.ShapeDtypeStruct(tile_shape, jnp.bfloat16),
            jax.ShapeDtypeStruct((bands * LANES,), jnp.int32),
        ),
        in_specs=[vmem] + [hbm] * 3,
        out_specs=(vmem, smem),
        scratch_shapes=[
            pltpu.VMEM((bands, rows), jnp.int32),
            pltpu.VMEM((bands, rows), jnp.int32),
            pltpu.VMEM((1, rows), jnp.int32),
            pltpu.VMEM((bands, LANES), jnp.int32),
            pltpu.SemaphoreType.DMA((3,)),
            pltpu.SemaphoreType.DMA((bands,)),
        ],
        compiler_params=params,
        cost_estimate=pl.CostEstimate(flops=1 << 20, bytes_accessed=2 << 20, transcendentals=0),
        name="locate",
    )(rounded, in_hbm(cols), in_hbm(mask), in_hbm(dest.T))

    def exchange(value, distances):
        pairs_of = [(place, place ^ distances[place % 2]) for place in range(devices)]
        return lax.ppermute(value, ("grp", "row"), pairs_of)

    def direct(value, steps):
        held = [value]
        for place in range(1, 1 << len(steps)):
            even = sum(step[0] for order, step in enumerate(steps) if place >> order & 1)
            odd = sum(step[1] for order, step in enumerate(steps) if place >> order & 1)
            held.append(exchange(value, (even, odd)))
        return held

    even, odd = levels(devices)
    count = 1 << len(even)

    def first_level(value, own):
        held = direct(value, list(zip(even, odd[::-1])))
        return jnp.concatenate([held[-1]] + held[1:-1] + [own], axis=0)

    def second_level(value, own):
        near = direct(value, list(zip(odd, even)))
        near, away = near[::-1], ([own] + near[1:])[::-1]
        plan = [(number, 0, count, number * count) for number in range(2 * count)]
        return plan, near + [exchange(part, (1, 1)) for part in away]

    def both_levels(value):
        ahead = direct(value, list(zip(even, odd[::-1])))
        copy = pl.pallas_call(
            duplicate,
            out_shape=jax.ShapeDtypeStruct(tile_shape, jnp.bfloat16),
            in_specs=[vmem],
            out_specs=vmem,
            compiler_params=params,
            name="duplicate",
        )(value)
        aside = direct(copy, list(zip(odd, even)))
        ahead = jnp.concatenate([ahead[-1]] + ahead[1:-1], axis=0)
        aside = jnp.concatenate([aside[-1]] + aside[1:-1] + [copy], axis=0)
        near = [aside, ahead] + direct(ahead, list(zip(odd, even)))[:0:-1]
        plan = []
        for core in range(2):
            base, number = core * count * count, core * len(near)
            for place in range(count):
                row = {0: 0, count - 1: count - 1}.get(place, count - 1 - place)
                plan.append((number, place, 1, base + row * count + count - 1))
            plan.append((number + 1, 0, count - 1, base + (count - 1) * count))
            for row in range(count - 1):
                plan.append((number + 2 + row, 0, count - 1, base + row * count))
        return plan, near + [exchange(part, (1, 1)) for part in near]

    gathered = first_level(rounded, own)
    own, x, right, smooth, blocks = pl.pallas_call(
        prepare,
        out_shape=(
            jax.ShapeDtypeStruct(gathered.shape, jnp.bfloat16),
            jax.ShapeDtypeStruct(tile_shape, jnp.float32),
            jax.ShapeDtypeStruct(tile_shape, jnp.bfloat16),
            jax.ShapeDtypeStruct((pairs, 2 * block, 2 * block), jnp.bfloat16),
            jax.ShapeDtypeStruct(coarse_blocks.shape, jnp.bfloat16),
        ),
        in_specs=[smem, vmem] + [hbm] * 3,
        out_specs=(vmem,) * 5,
        scratch_shapes=[
            pltpu.VMEM(smoother.shape, jnp.bfloat16),
            pltpu.VMEM(residual.shape, jnp.bfloat16),
            pltpu.VMEM((smooth_rows, LANES), jnp.float32),
            pltpu.VMEM((right_rows, LANES), jnp.float32),
            pltpu.VMEM((pairs * LANES, LANES), jnp.float32),
            pltpu.SemaphoreType.DMA((3,)),
        ],
        compiler_params=params,
        cost_estimate=pl.CostEstimate(flops=1 << 26, bytes_accessed=10 << 20, transcendentals=0),
        name="prepare",
    )(perm, gathered, in_hbm(smoother), in_hbm(residual), in_hbm(coarse_blocks))

    def sweep(x, plan, pieces, last):
        outs = [jax.ShapeDtypeStruct(tile_shape, jnp.float32)]
        if not last:
            outs.append(jax.ShapeDtypeStruct(tile_shape, jnp.bfloat16))
        return pl.pallas_call(
            functools.partial(later_sweep, plan, len(pieces), not last),
            out_shape=tuple(outs),
            in_specs=[smem, smem] + [vmem] * (len(pieces) + 4),
            out_specs=tuple([vmem] * len(outs)),
            scratch_shapes=[
                pltpu.VMEM((devices * pairs + 1, NRHS, LANES), jnp.bfloat16),
                pltpu.VMEM(tile_shape, jnp.bfloat16),
            ],
            compiler_params=params,
            name="later_sweep",
        )(perm, index, *pieces, blocks, smooth, right, x)

    x, rounded = sweep(x, *second_level(gathered, own), False)
    (x,) = sweep(x, *both_levels(rounded), True)

    if not full:
        flat = x.reshape(rows, NRHS * block)
        following = jnp.concatenate([starts[1:], jnp.full((1,), rows, jnp.int32)])
        slots = devices * CAP
        wanted = starts[:, None] + jnp.arange(CAP, dtype=jnp.int32)[None, :]
        live = wanted < following[:, None]
        flat = jnp.where(
            live.reshape(slots, 1), jnp.take(flat, wanted.reshape(slots), axis=0, mode="clip"), 0.0
        )
        x = flat.reshape(devices, NRHS, LANES)
    got = lax.all_to_all(x, ("grp", "row"), split_axis=0, concat_axis=0, tiled=True)
    return pl.pallas_call(
        lay_out,
        out_shape=jax.ShapeDtypeStruct((devices * CAP, NRHS * block), jnp.float32),
        in_specs=[vmem],
        out_specs=vmem,
        compiler_params=params,
        name="lay_out",
    )(got.reshape(devices * NRHS, LANES))


def solution(mesh):
    in_specs = (
        P(("grp", "row"), None, None),
        P(("grp", "row"), None),
        P(("grp", "row"), None),
        P(("grp", "row"), None),
        P(("grp", "row"), None),
        P(("grp", "row"), None),
    )
    out_specs = P(("grp", "row"), None)
    return jax.shard_map(local, mesh=mesh, in_specs=in_specs, out_specs=out_specs, check_vma=False)
```

```python
import functools

import jax
import jax.numpy as jnp
from jax import lax
from jax.experimental import pallas as pl
from jax.experimental.pallas import tpu as pltpu
from jax.sharding import PartitionSpec as P

NRHS = 8
CAP = 2
LANES = 128
VMEM_LIMIT = 32 * 1024 * 1024

TRANSPOSED = (((1,), (1,)), ((), ()))
PLAIN = (((1,), (0,)), ((), ()))
SUB = 8


def spread_rows(source_ref, spread_ref, copies):
    rows, width = source_ref.shape
    tiles = width // LANES
    for top in range(rows // SUB):
        values = source_ref[top * SUB : (top + 1) * SUB, :].astype(jnp.float32)
        for place, (tile, turned) in enumerate(copies):
            piece = values[:, tile * LANES : (tile + 1) * LANES]
            if turned:
                piece = pltpu.roll(piece, LANES // 2, 1)
            spread_ref[pl.ds((top * len(copies) + place) * SUB, SUB), :] = piece


def spread_row(spread_ref, row, tiles, first, count):
    start = (row // SUB) * (tiles * SUB) + first * SUB + row % SUB
    return spread_ref[pl.ds(start, count, stride=SUB), :]


def smooth_copies(width):
    return [(tile, False) for tile in range(width // LANES)]


def right_copies(width):
    plain = [(tile, False) for tile in range(width // LANES)]
    turned = [(tile, True) for tile in range(width // LANES)]
    return plain + turned + plain


def sort_rows(full, dest_ref, perm_ref, starts_ref, count):
    rows = dest_ref.shape[0]
    owners = starts_ref.shape[0]
    if full:
        for owner in range(owners):
            count[owner] = owner * CAP
            starts_ref[owner] = owner * CAP
    else:

        def clear(owner, carry):
            count[owner] = 0
            return carry

        lax.fori_loop(0, owners, clear, 0)

        def tally(row, carry):
            count[dest_ref[row]] = count[dest_ref[row]] + 1
            return carry

        lax.fori_loop(0, rows, tally, 0)

        def start(owner, total):
            following = total + count[owner]
            starts_ref[owner] = total
            count[owner] = total
            return following

        lax.fori_loop(0, owners, start, jnp.int32(0))
    for row in range(rows):
        owner = dest_ref[row]
        position = count[owner]
        count[owner] = position + 1
        perm_ref[position] = row


def first_sweep(
    full, dest_hbm, smooth_hbm, right_hbm, perm_ref, starts_ref, xb_ref,
    dest_ref, count, smooth_ref, right_ref, smooth_spread, right_spread, collected, sems,
):
    copies = [
        pltpu.make_async_copy(dest_hbm, dest_ref, sems.at[0]),
        pltpu.make_async_copy(right_hbm, right_ref, sems.at[1]),
        pltpu.make_async_copy(smooth_hbm, smooth_ref, sems.at[2]),
    ]
    for copy in copies:
        copy.start()
    rows, smooth_width = smooth_ref.shape
    block = LANES // 2
    half = smooth_width // LANES
    quad = LANES // half
    lanes = lax.broadcasted_iota(jnp.int32, (2 * SUB, LANES), 1)
    lower = lanes[:SUB] < block
    width = quad * block
    held = lax.broadcasted_iota(jnp.int32, (width, width), 0)
    wanted = lax.broadcasted_iota(jnp.int32, (width, width), 1)
    placed = ((held % LANES) // half) * block + 2 * (held % half) + held // LANES
    order = jnp.where(placed == wanted, 1.0, 0.0).astype(jnp.bfloat16)

    copies[0].wait()
    sort_rows(full, dest_ref, perm_ref, starts_ref, count)
    copies[1].wait()
    copied = right_copies(right_ref.shape[1])
    spread_rows(right_ref, right_spread, copied)
    copies[2].wait()
    spread_rows(smooth_ref, smooth_spread, smooth_copies(smooth_width))

    for group in range(rows // quad):
        weights, values = [], []
        for member in range(quad):
            row = perm_ref[quad * group + member]
            weights.append(spread_row(smooth_spread, row, half, 0, half))
            straight = spread_row(right_spread, row, len(copied), 0, SUB)
            crossed = spread_row(right_spread, row, len(copied), SUB // 2, SUB)
            values += [jnp.where(lower, straight, 0.0), jnp.where(lower, 0.0, crossed)]
        products = lax.dot_general(
            jnp.concatenate(values, axis=0).astype(jnp.bfloat16),
            jnp.concatenate(weights, axis=0).astype(jnp.bfloat16),
            TRANSPOSED,
            preferred_element_type=jnp.float32,
        )
        own = products[: 2 * SUB]
        for member in range(1, quad):
            own = jnp.where(
                lanes // half == member, products[2 * SUB * member : 2 * SUB * (member + 1)], own
            )
        collected[pl.ds(group * SUB, SUB), :LANES] = own[:SUB]
        collected[pl.ds(group * SUB, SUB), LANES:] = own[SUB:]
    ordered = lax.dot_general(
        collected[...].astype(jnp.bfloat16), order, PLAIN, preferred_element_type=jnp.float32
    ).astype(jnp.bfloat16)
    for group in range(rows // quad):
        for pair in range(quad // 2):
            xb_ref[group * (quad // 2) + pair] = ordered[
                group * SUB : (group + 1) * SUB, pair * LANES : (pair + 1) * LANES
            ]


def levels(devices):
    distances = [1 << bit for bit in range(1, devices.bit_length() - 1)]
    half = len(distances) // 2
    return distances[:half][::-1], distances[half:]


def find_tiles(devices, members, pairs, cols, mask, dest, own):
    slots = devices * CAP
    rank = cols % CAP
    source = (cols % slots) // CAP
    position = ((dest // members) * members + cols // slots) * CAP + rank
    return place_tiles(devices, pairs, source, position, mask, own)


def place_tiles(devices, pairs, source, position, mask, own):
    relative = source ^ own

    def collect(distances):
        return sum(((relative // distance) % 2) * (1 << order) for order, distance in enumerate(distances))

    near, far = levels(devices)
    count = 1 << len(near)
    even = source % 2 == 0
    piece = count - 1 - jnp.where(even, collect(far), collect(near))
    within = jnp.where(even, collect(near), collect(far[::-1]))
    within = jnp.where(within == 0, count - 1, jnp.where(within == count - 1, 0, within))
    tile = (((relative % 2) * count + piece) * count + within) * pairs + position // 2
    swap = (position + lax.broadcasted_iota(jnp.int32, position.shape, 0)) % 2
    return jnp.where(mask != 0, tile * 2 + swap, 2 * devices * pairs)


def in_hbm(value):
    return pltpu.with_memory_space_constraint(value, pltpu.HBM)


def locate(
    full, devices, members, rounded_ref, cols_hbm, mask_hbm, dest_hbm, own_ref, index_ref,
    cols_ref, mask_ref, dest_ref, lined, sems, line_sems,
):
    moves = [(cols_hbm, cols_ref), (mask_hbm, mask_ref), (dest_hbm, dest_ref)]
    copies = [pltpu.make_async_copy(*move, sems.at[number]) for number, move in enumerate(moves)]
    for copy in copies:
        copy.start()
    own_ref[...] = rounded_ref[...]
    for copy in copies:
        copy.wait()
    bands, rows = cols_ref.shape
    places = cols_ref[...]
    if full:
        places = find_tiles(
            devices, members, rows // 2, places, mask_ref[...], dest_ref[...],
            lax.axis_index("grp") * members + lax.axis_index("row"),
        )
    lined[:, :rows] = places
    lines = [
        pltpu.make_async_copy(lined.at[band], index_ref.at[pl.ds(band * LANES, LANES)], line_sems.at[band])
        for band in range(bands)
    ]
    for line in lines:
        line.start()
    for line in lines:
        line.wait()


def prepare(
    perm_ref, gathered_ref, smooth_hbm, right_hbm, blocks_hbm, own_ref, x_ref, rp_ref, sbd_ref, blocks_ref,
    smooth_ref, right_ref, smooth_spread, right_spread, widened, sems,
):
    moves = [(right_hbm, right_ref), (smooth_hbm, smooth_ref), (blocks_hbm, blocks_ref)]
    copies = [pltpu.make_async_copy(*move, sems.at[number]) for number, move in enumerate(moves)]
    for copy in copies:
        copy.start()
    own_ref[...] = gathered_ref[...]
    rows, smooth_width = smooth_ref.shape
    block = LANES // 2
    half = smooth_width // LANES
    pairs = rows // 2
    lower = lax.broadcasted_iota(jnp.int32, (SUB, LANES), 1) < block
    low_half = lax.broadcasted_iota(jnp.int32, (half, LANES), 1) < block
    copies[0].wait()
    copied = right_copies(right_ref.shape[1])
    spread_rows(right_ref, right_spread, copied)
    copies[1].wait()
    spread_rows(smooth_ref, smooth_spread, smooth_copies(smooth_width))
    for pair in range(pairs):
        low, high = perm_ref[2 * pair], perm_ref[2 * pair + 1]
        rp_ref[pair] = jnp.where(
            lower,
            spread_row(right_spread, low, len(copied), 0, SUB),
            spread_row(right_spread, high, len(copied), SUB // 2, SUB),
        ).astype(jnp.bfloat16)
        base = pair * LANES
        for number, row in enumerate((low, high)):
            straight = spread_row(smooth_spread, row, half, 0, half)
            turned = pltpu.roll(straight, block, 1)
            first, second = (straight, turned) if number == 0 else (turned, straight)
            keep = low_half if number == 0 else jnp.logical_not(low_half)
            widened[pl.ds(base + number * block, half, stride=2), :] = jnp.where(keep, first, 0.0)
            widened[pl.ds(base + number * block + 1, half, stride=2), :] = jnp.where(keep, second, 0.0)
    for pair in range(pairs):
        sbd_ref[pair] = widened[pl.ds(pair * LANES, LANES), :].T.astype(jnp.bfloat16)
    for pair in range(pairs):
        x_ref[pair] = lax.dot_general(
            rp_ref[pair], sbd_ref[pair], PLAIN, preferred_element_type=jnp.float32
        )
    copies[2].wait()


def later_sweep(plan, piece_count, with_rounded, *refs):
    perm_ref, index_ref = refs[:2]
    pieces = refs[2 : 2 + piece_count]
    blocks, sbd_ref, rp_ref, x_ref = refs[2 + piece_count : 6 + piece_count]
    refs = refs[6 + piece_count :]
    out_ref = refs[0]
    rounded_ref = refs[1] if with_rounded else None
    tiles, defects = refs[2 if with_rounded else 1 :]
    pairs = x_ref.shape[0]
    rows, block, width = blocks.shape
    bands = width // block

    for number, start, size, place in plan:
        tiles[pl.ds(place * pairs, size * pairs)] = pieces[number][pl.ds(start * pairs, size * pairs)]
    tiles[tiles.shape[0] - 1] = jnp.zeros((NRHS, LANES), jnp.bfloat16)

    lower = lax.broadcasted_iota(jnp.int32, (NRHS, LANES), 1) < block

    first_half = lax.broadcasted_iota(jnp.int32, (NRHS, LANES), 0) < NRHS // 2

    def fetch(row, band):
        entry = index_ref[band * LANES + row]
        tile = tiles[lax.shift_right_logical(entry, 1)].astype(jnp.float32)
        return pltpu.roll(tile, (entry & 1) * block, 1)

    def values(row):
        return [
            jnp.where(lower, fetch(row, 2 * half), fetch(row, 2 * half + 1)) for half in range(bands // 2)
        ]

    for quad in range(rows // 4):
        members = [perm_ref[4 * quad + member] for member in range(4)]
        gathered = jnp.concatenate([jnp.concatenate(values(row), axis=1) for row in members], axis=0)
        weights = jnp.concatenate([blocks[row] for row in members], axis=0)
        applied = lax.dot_general(
            gathered.astype(jnp.bfloat16), weights, TRANSPOSED, preferred_element_type=jnp.float32
        )
        for half in range(2):
            pair = 2 * quad + half
            own = applied[2 * NRHS * half : 2 * NRHS * (half + 1), LANES * half : LANES * (half + 1)]
            image = jnp.where(lower, own[:NRHS], own[NRHS:])
            defects[pair] = (rp_ref[pair].astype(jnp.float32) - image).astype(jnp.bfloat16)

    for pair in range(pairs):
        x = x_ref[pair] + lax.dot_general(
            defects[pair], sbd_ref[pair], PLAIN, preferred_element_type=jnp.float32
        )
        if with_rounded:
            out_ref[pair] = x
            rounded_ref[pair] = x.astype(jnp.bfloat16)
        else:
            crossed = pltpu.roll(pltpu.roll(x, block, 1), NRHS // 2, 0)
            out_ref[pair] = jnp.where(lower == first_half, x, crossed)


def lay_out(got_ref, out_ref):
    rows, width = out_ref.shape
    tiles = width // LANES
    for tile in range(tiles):
        out_ref[:, tile * LANES : (tile + 1) * LANES] = got_ref[pl.ds(tile, rows, stride=tiles), :]


def local(coarse_blocks, smoother, residual, dest, band_cols, band_mask):
    groups = lax.axis_size("grp")
    members = lax.axis_size("row")
    devices = groups * members
    rows, block, width = coarse_blocks.shape
    bands = band_cols.shape[1]
    pairs = rows // 2
    full = rows == devices * CAP
    smem = pl.BlockSpec(memory_space=pltpu.SMEM)
    vmem = pl.BlockSpec(memory_space=pltpu.VMEM)
    hbm = pl.BlockSpec(memory_space=pltpu.HBM)
    tile_shape = (pairs, NRHS, LANES)
    params = pltpu.CompilerParams(vmem_limit_bytes=VMEM_LIMIT)

    smooth_width, right_width = smoother.shape[1], residual.shape[1]
    smooth_rows = rows * len(smooth_copies(smooth_width))
    right_rows = rows * len(right_copies(right_width))
    perm, starts, rounded = pl.pallas_call(
        functools.partial(first_sweep, full),
        out_shape=(
            jax.ShapeDtypeStruct((rows,), jnp.int32),
            jax.ShapeDtypeStruct((devices,), jnp.int32),
            jax.ShapeDtypeStruct(tile_shape, jnp.bfloat16),
        ),
        in_specs=[hbm] * 3,
        out_specs=(smem, smem, vmem),
        scratch_shapes=[
            pltpu.SMEM((rows,), jnp.int32),
            pltpu.SMEM((devices,), jnp.int32),
            pltpu.VMEM(smoother.shape, jnp.bfloat16),
            pltpu.VMEM(residual.shape, jnp.bfloat16),
            pltpu.VMEM((smooth_rows, LANES), jnp.float32),
            pltpu.VMEM((right_rows, LANES), jnp.float32),
            pltpu.VMEM((pairs * SUB // 2, 2 * LANES), jnp.float32),
            pltpu.SemaphoreType.DMA((3,)),
        ],
        compiler_params=params,
        name="first_sweep",
    )(in_hbm(dest.reshape(rows)), in_hbm(smoother), in_hbm(residual))
    cols, mask = band_cols.T, band_mask.T
    if not full:
        slots = devices * CAP
        table = lax.all_gather(starts, ("grp", "row"), axis=0, tiled=True)
        source = (cols % slots) // CAP
        owner = (dest.T // members) * members + cols // slots
        position = jnp.take(table, source * devices + owner, mode="clip") + cols % CAP
        cols = place_tiles(devices, pairs, source, position, mask, lax.axis_index(("grp", "row")))
    own, index = pl.pallas_call(
        functools.partial(locate, full, devices, members),
        out_shape=(
            jax.ShapeDtypeStruct(tile_shape, jnp.bfloat16),
            jax.ShapeDtypeStruct((bands * LANES,), jnp.int32),
        ),
        in_specs=[vmem] + [hbm] * 3,
        out_specs=(vmem, smem),
        scratch_shapes=[
            pltpu.VMEM((bands, rows), jnp.int32),
            pltpu.VMEM((bands, rows), jnp.int32),
            pltpu.VMEM((1, rows), jnp.int32),
            pltpu.VMEM((bands, LANES), jnp.int32),
            pltpu.SemaphoreType.DMA((3,)),
            pltpu.SemaphoreType.DMA((bands,)),
        ],
        compiler_params=params,
        cost_estimate=pl.CostEstimate(flops=1 << 20, bytes_accessed=2 << 20, transcendentals=0),
        name="locate",
    )(rounded, in_hbm(cols), in_hbm(mask), in_hbm(dest.T))

    def exchange(value, distances):
        pairs_of = [(place, place ^ distances[place % 2]) for place in range(devices)]
        return lax.ppermute(value, ("grp", "row"), pairs_of)

    def direct(value, steps):
        held = [value]
        for place in range(1, 1 << len(steps)):
            even = sum(step[0] for order, step in enumerate(steps) if place >> order & 1)
            odd = sum(step[1] for order, step in enumerate(steps) if place >> order & 1)
            held.append(exchange(value, (even, odd)))
        return held

    even, odd = levels(devices)
    count = 1 << len(even)

    def first_level(value, own):
        held = direct(value, list(zip(even, odd[::-1])))
        return jnp.concatenate([held[-1]] + held[1:-1] + [own], axis=0)

    def second_level(value, own):
        near = direct(value, list(zip(odd, even)))
        near, away = near[::-1], ([own] + near[1:])[::-1]
        plan = [(number, 0, count, number * count) for number in range(2 * count)]
        return plan, near + [exchange(part, (1, 1)) for part in away]

    def both_levels(value):
        ahead = direct(value, list(zip(even, odd[::-1])))
        aside = direct(value, list(zip(odd, even)))
        ahead = jnp.concatenate([ahead[-1]] + ahead[1:-1], axis=0)
        aside = jnp.concatenate([aside[-1]] + aside[1:-1] + [value], axis=0)
        near = [aside, ahead] + direct(ahead, list(zip(odd, even)))[:0:-1]
        plan = []
        for core in range(2):
            base, number = core * count * count, core * len(near)
            for place in range(count):
                row = {0: 0, count - 1: count - 1}.get(place, count - 1 - place)
                plan.append((number, place, 1, base + row * count + count - 1))
            plan.append((number + 1, 0, count - 1, base + (count - 1) * count))
            for row in range(count - 1):
                plan.append((number + 2 + row, 0, count - 1, base + row * count))
        return plan, near + [exchange(part, (1, 1)) for part in near]

    gathered = first_level(rounded, own)
    own, x, right, smooth, blocks = pl.pallas_call(
        prepare,
        out_shape=(
            jax.ShapeDtypeStruct(gathered.shape, jnp.bfloat16),
            jax.ShapeDtypeStruct(tile_shape, jnp.float32),
            jax.ShapeDtypeStruct(tile_shape, jnp.bfloat16),
            jax.ShapeDtypeStruct((pairs, 2 * block, 2 * block), jnp.bfloat16),
            jax.ShapeDtypeStruct(coarse_blocks.shape, jnp.bfloat16),
        ),
        in_specs=[smem, vmem] + [hbm] * 3,
        out_specs=(vmem,) * 5,
        scratch_shapes=[
            pltpu.VMEM(smoother.shape, jnp.bfloat16),
            pltpu.VMEM(residual.shape, jnp.bfloat16),
            pltpu.VMEM((smooth_rows, LANES), jnp.float32),
            pltpu.VMEM((right_rows, LANES), jnp.float32),
            pltpu.VMEM((pairs * LANES, LANES), jnp.float32),
            pltpu.SemaphoreType.DMA((3,)),
        ],
        compiler_params=params,
        cost_estimate=pl.CostEstimate(flops=1 << 26, bytes_accessed=10 << 20, transcendentals=0),
        name="prepare",
    )(perm, gathered, in_hbm(smoother), in_hbm(residual), in_hbm(coarse_blocks))

    def sweep(x, plan, pieces, last):
        outs = [jax.ShapeDtypeStruct(tile_shape, jnp.float32)]
        if not last:
            outs.append(jax.ShapeDtypeStruct(tile_shape, jnp.bfloat16))
        return pl.pallas_call(
            functools.partial(later_sweep, plan, len(pieces), not last),
            out_shape=tuple(outs),
            in_specs=[smem, smem] + [vmem] * (len(pieces) + 4),
            out_specs=tuple([vmem] * len(outs)),
            scratch_shapes=[
                pltpu.VMEM((devices * pairs + 1, NRHS, LANES), jnp.bfloat16),
                pltpu.VMEM(tile_shape, jnp.bfloat16),
            ],
            compiler_params=params,
            name="later_sweep",
        )(perm, index, *pieces, blocks, smooth, right, x)

    x, rounded = sweep(x, *second_level(gathered, own), False)
    (x,) = sweep(x, *both_levels(rounded), True)

    if not full:
        flat = x.reshape(rows, NRHS * block)
        following = jnp.concatenate([starts[1:], jnp.full((1,), rows, jnp.int32)])
        slots = devices * CAP
        wanted = starts[:, None] + jnp.arange(CAP, dtype=jnp.int32)[None, :]
        live = wanted < following[:, None]
        flat = jnp.where(
            live.reshape(slots, 1), jnp.take(flat, wanted.reshape(slots), axis=0, mode="clip"), 0.0
        )
        x = flat.reshape(devices, NRHS, LANES)
    got = lax.all_to_all(x, ("grp", "row"), split_axis=0, concat_axis=0, tiled=True)
    return pl.pallas_call(
        lay_out,
        out_shape=jax.ShapeDtypeStruct((devices * CAP, NRHS * block), jnp.float32),
        in_specs=[vmem],
        out_specs=vmem,
        compiler_params=params,
        name="lay_out",
    )(got.reshape(devices * NRHS, LANES))


def solution(mesh):
    in_specs = (
        P(("grp", "row"), None, None),
        P(("grp", "row"), None),
        P(("grp", "row"), None),
        P(("grp", "row"), None),
        P(("grp", "row"), None),
        P(("grp", "row"), None),
    )
    out_specs = P(("grp", "row"), None)
    return jax.shard_map(local, mesh=mesh, in_specs=in_specs, out_specs=out_specs, check_vma=False)
```
